32 devices in a mesh: groups: 2 (over y), replica: 4 (over z), tensor: 4 (over x, core).
Axes of the slice: x: 2, y: 2, z: 4, core: 2. Of those that a mesh axis runs over, the one named last changes fastest.
Arguments:
- queries: bfloat16 [2048, 4096], P(('groups', 'replica'), 'tensor'), parts along dimension 0
- fresh_key_value: bfloat16 [2048, 1024], P(('groups', 'replica')), parts along dimension 0, may hold values from -6 to 6
- key_value_cache_blocks: bfloat16 [1024, 16, 1024], P(('groups', 'replica')), parts along dimension 0
- row_block_indices: int32 [2048, 16], P(('groups', 'replica')), parts along dimension 0, may hold values from 0 to 127
- cached_length: int32 [2048], P(('groups', 'replica')), parts along dimension 0, may hold values from 1 to 256
- row_adapter_id: int32 [2048], P(('groups', 'replica')), parts along dimension 0, may hold values from 0 to 7
- adapter_storage_slot: int32 [8], replicated, may hold values from 0 to 7, each once
- leaving_row_indices: int32 [8, 2], P(('groups', 'replica')), parts along dimension 0, may hold values from 0 to 255, as said below
- receiving_replica: int32 [8], P(('groups', 'replica')), parts along dimension 0, may hold values from 0 to 3, each once
- output_weight_matrix: bfloat16 [4096, 8192], P('tensor'), may hold values from -0.09375 to 0.09375
- adapter_down_weight: bfloat16 [8, 4096, 64], P('replica', 'tensor'), may hold values from -0.09375 to 0.09375
- adapter_up_weight: bfloat16 [8, 64, 8192], P('replica', None, 'tensor'), may hold values from -0.75 to 0.75
Outputs:
- mixed: bfloat16 [2048, 8192], P(('groups', 'replica'), 'tensor'), parts along dimension 0
The draws below stay inside these ranges and needn't reach their ends.
There are 2 independent parts, one for each index of `groups`. The reference program is written for one: setup_inputs(seed, part) draws one part's arguments, and reference() takes and returns one part's arrays. A program takes and returns all parts, laid end to end along the dimension named above; an argument that names none is the same for every part. Nothing has to cross between parts.
Inputs may be any that keep to these rules, and one draw needn't show every extreme that they name: `leaving_row_indices`: each replica's 2 entries are distinct.
All inputs are finite; a program needn't handle non-finite values.
Results may differ from the reference program's by a relative error of at most 0.008.
Values may be sent and summed in bfloat16 or wider, within the bound.
No kernel may reach another device: no remote copies, remote signals or barrier semaphores. Data moves between devices by JAX's collectives and lax.ppermute only.
A program may use at most 128 MiB of HBM per device.

```python
import math
import jax
import jax.numpy as jnp
import numpy as np
from jax import lax

MODEL_WIDTH = 8192
QUERY_HEADS_HALF = 32
KVH = 4
HEAD_SIZE = 128
ADAPTER_RANK = 64
BS = 16
MAXB = 16
ROWS = 256
NBLK = 128
MOVE = 2
CTX = 256
TOTAL = 1024
BLOCKS = 512
ADAPTER_COUNT = 8
N_REPLICA = 4


def draw_queries(key, part):
    key = jax.random.fold_in(key, 3)
    values = jax.random.normal(key, (TOTAL, QUERY_HEADS_HALF * HEAD_SIZE), jnp.float32)
    return jnp.clip(values, -6.0, 6.0).astype(jnp.bfloat16)


def draw_key_value_cache_blocks(key, part):
    key = jax.random.fold_in(key, 5)
    values = jax.random.normal(key, (BLOCKS, BS, KVH * 2 * HEAD_SIZE), jnp.float32)
    return jnp.clip(values, -6.0, 6.0).astype(jnp.bfloat16)


def draw_leaving_row_indices(key, part):
    key = jax.random.fold_in(key, 11)
    replica_keys = jax.random.split(key, N_REPLICA)
    picks = jax.vmap(lambda single: jax.random.permutation(single, ROWS)[:MOVE])(replica_keys).astype(jnp.int32)
    chosen_replica = jax.random.randint(jax.random.fold_in(key, 1), (), 0, N_REPLICA)
    others = 1 + jax.random.permutation(jax.random.fold_in(key, 2), ROWS - 2)[:MOVE - 2].astype(jnp.int32)
    edges = jnp.array([0, ROWS - 1], jnp.int32)
    special = jnp.concatenate([edges, others])
    replica_ids = jnp.arange(N_REPLICA, dtype=jnp.int32)[:, None]
    return jnp.where(replica_ids == chosen_replica, special[None, :], picks).astype(jnp.int32)


def set_ends(result, stream_key, smallest, largest):
    spot = [jax.random.randint(jax.random.fold_in(stream_key, axis), (), 0, length) for axis, length in enumerate(result.shape)]
    main_axis = result.shape.index(max(result.shape))
    next_to = spot[:main_axis] + [(spot[main_axis] + 1) % result.shape[main_axis]] + spot[main_axis + 1:]
    return result.at[tuple(spot)].set(smallest).at[tuple(next_to)].set(largest)


def level_of(stream_key, dims, pieces, least, largest):
    factor_of, own = 1.0, jax.random.fold_in(stream_key, 6)
    for axis_at, parts in pieces:
        draws = jnp.exp(jax.random.uniform(jax.random.fold_in(own, axis_at), (parts,), jnp.float32, least / len(pieces), largest / len(pieces)))
        factor_of = factor_of * jnp.repeat(draws, dims[axis_at] // parts).reshape([-1 if axis == axis_at else 1 for axis in range(len(dims))])
    return factor_of


def rank_bounds(number_of, slope):
    weights = [(1 << 20) // math.isqrt(rank ** slope) + 1 for rank in range(1, number_of + 1)]
    scale = 1 + sum(weights) // (1 << 30)
    return np.cumsum(np.array([max(1, weight // scale) for weight in weights]))


def ranked_ids(own_key, shape, count, lean):
    listing = rank_bounds(count, lean)
    pick = jax.random.randint(jax.random.fold_in(own_key, 1), shape, 0, int(listing[count - 1]))
    standing = jnp.searchsorted(jnp.asarray(listing, jnp.int32), pick, side="right")
    return jax.random.permutation(jax.random.fold_in(own_key, 2), count)[standing].astype(jnp.int32)


def gaussian(own_key, shape, spread, limit, cuts=(), kind=jnp.bfloat16):
    values = spread * jax.random.normal(own_key, shape, jnp.float32)
    if cuts:
        values = values * level_of(own_key, shape, cuts, -0.22, 0.18)
    return jnp.clip(values, -limit, limit).astype(kind)


def setup_inputs(seed: int = 0, part: int = 0) -> dict:
    arg_keys = jax.random.split(jax.random.key(seed), 13)
    own_keys = jax.random.split(jax.random.fold_in(arg_keys[12], part), 13)
    queries = draw_queries(jax.random.fold_in(jax.random.fold_in(arg_keys[12], part), 71), part)
    fresh_key_value = gaussian(own_keys[1], (TOTAL, KVH * 2 * HEAD_SIZE), 1.0, 6.0, ((0, 4),))
    key_value_cache_blocks = draw_key_value_cache_blocks(jax.random.fold_in(jax.random.fold_in(arg_keys[12], part), 71), part)
    row_block_indices = set_ends(jax.random.randint(own_keys[3], (TOTAL, MAXB), 0, NBLK), jax.random.fold_in(own_keys[3], 1), 0, NBLK - 1).astype(jnp.int32)
    cached_length = set_ends(jax.random.randint(own_keys[4], (TOTAL,), 1, CTX + 1), jax.random.fold_in(own_keys[4], 1), 1, CTX).astype(jnp.int32)
    row_adapter_id = set_ends(ranked_ids(own_keys[5], (TOTAL,), ADAPTER_COUNT, 2), jax.random.fold_in(own_keys[5], 3), 0, ADAPTER_COUNT - 1).astype(jnp.int32)
    adapter_storage_slot = jax.random.permutation(arg_keys[6], ADAPTER_COUNT).astype(jnp.int32)
    leaving_row_indices = draw_leaving_row_indices(jax.random.fold_in(jax.random.fold_in(arg_keys[12], part), 71), part)
    receiving_replica = jax.random.permutation(own_keys[8], N_REPLICA).astype(jnp.int32)
    output_weight_matrix = gaussian(arg_keys[9], (QUERY_HEADS_HALF * HEAD_SIZE, MODEL_WIDTH), (QUERY_HEADS_HALF * HEAD_SIZE) ** -0.5, 0.09375, ((0, 4),))
    adapter_down_weight = gaussian(arg_keys[10], (ADAPTER_COUNT, QUERY_HEADS_HALF * HEAD_SIZE, ADAPTER_RANK), (QUERY_HEADS_HALF * HEAD_SIZE) ** -0.5, 0.09375, ((0, 4), (1, 4)))
    adapter_up_weight = gaussian(arg_keys[11], (ADAPTER_COUNT, ADAPTER_RANK, MODEL_WIDTH), ADAPTER_RANK ** -0.5, 0.75, ((0, 4), (2, 4)))
    return dict(queries=queries, fresh_key_value=fresh_key_value, key_value_cache_blocks=key_value_cache_blocks, row_block_indices=row_block_indices, cached_length=cached_length, row_adapter_id=row_adapter_id, adapter_storage_slot=adapter_storage_slot, leaving_row_indices=leaving_row_indices, receiving_replica=receiving_replica, output_weight_matrix=output_weight_matrix, adapter_down_weight=adapter_down_weight, adapter_up_weight=adapter_up_weight)


adapter_scale = 2.0

def reference(queries, fresh_key_value, key_value_cache_blocks, row_block_indices, cached_length, row_adapter_id, adapter_storage_slot, leaving_row_indices, receiving_replica, output_weight_matrix, adapter_down_weight, adapter_up_weight):
    group_size = QUERY_HEADS_HALF // KVH
    score_scale = 1.0 / math.sqrt(HEAD_SIZE)

    def serve(replica_number):
        begin_row = (replica_number * ROWS).astype(jnp.int32)
        query_rows = lax.dynamic_slice_in_dim(queries, begin_row, ROWS, 0)
        own_rows = lax.dynamic_slice_in_dim(fresh_key_value, begin_row, ROWS, 0)
        table_rows = lax.dynamic_slice_in_dim(row_block_indices, begin_row, ROWS, 0) + (replica_number * NBLK).astype(jnp.int32)
        lengths = lax.dynamic_slice_in_dim(cached_length, begin_row, ROWS, 0)
        adapters = lax.dynamic_slice_in_dim(row_adapter_id, begin_row, ROWS, 0)
        cache = key_value_cache_blocks[table_rows].reshape(ROWS, CTX, KVH, 2 * HEAD_SIZE).astype(jnp.float32)
        query_heads = query_rows.reshape(ROWS, KVH, group_size, HEAD_SIZE).astype(jnp.float32)
        own_heads = own_rows.reshape(ROWS, KVH, 2 * HEAD_SIZE).astype(jnp.float32)
        scores = jnp.einsum('nsgd,ncsd->nsgc', query_heads, cache[..., :HEAD_SIZE]) * score_scale
        is_valid = jnp.arange(CTX, dtype=jnp.int32)[None, :] < lengths[:, None]
        scores = jnp.where(is_valid[:, None, None, :], scores, -jnp.inf)
        own_score = jnp.einsum('nsgd,nsd->nsg', query_heads, own_heads[..., :HEAD_SIZE]) * score_scale
        row_max = jnp.maximum(lax.optimization_barrier(jnp.max(scores, axis=3)), own_score)
        weights_past = jnp.exp(scores - row_max[..., None])
        weight_own = jnp.exp(own_score - row_max)
        denominator = lax.optimization_barrier(jnp.sum(weights_past, axis=3)) + weight_own
        mixed_past = (weights_past / denominator[..., None]).astype(jnp.bfloat16).astype(jnp.float32)
        mixed_own = (weight_own / denominator).astype(jnp.bfloat16).astype(jnp.float32)
        attn = jnp.einsum('nsgc,ncsd->nsgd', mixed_past, cache[..., HEAD_SIZE:]) + mixed_own[..., None] * own_heads[:, :, None, HEAD_SIZE:]
        attn = attn.reshape(ROWS, QUERY_HEADS_HALF * HEAD_SIZE).astype(jnp.bfloat16)
        storage_slot_index = adapter_storage_slot[adapters]
        down_weight_rows = adapter_down_weight[storage_slot_index].astype(jnp.float32)
        shrunk = jnp.einsum('nk,nkr->nr', attn.astype(jnp.float32), down_weight_rows).astype(jnp.bfloat16)
        up_weight_rows = adapter_up_weight[storage_slot_index].astype(jnp.float32)
        frozen_projection_sum = jnp.dot(attn, output_weight_matrix, preferred_element_type=jnp.float32)
        adapter_update = jnp.einsum('nr,nrc->nc', shrunk.astype(jnp.float32), up_weight_rows)
        return (frozen_projection_sum + adapter_scale * adapter_update).astype(jnp.bfloat16)
    results = lax.map(serve, jnp.arange(N_REPLICA, dtype=jnp.int32))
    inverse = jnp.zeros((N_REPLICA,), jnp.int32).at[receiving_replica].set(jnp.arange(N_REPLICA, dtype=jnp.int32))
    targets = jnp.arange(N_REPLICA, dtype=jnp.int32)[:, None]
    arriving = results[inverse[:, None], leaving_row_indices[inverse]]
    placed = results.at[targets, leaving_row_indices].set(arriving)
    return placed.reshape(TOTAL, MODEL_WIDTH)
```

```python
import functools
import math

import jax
import jax.numpy as jnp
from jax import lax
from jax.experimental import pallas as pl
from jax.experimental.pallas import tpu as pltpu
from jax.sharding import PartitionSpec as P

QUERY_HEADS_HALF = 32
KVH = 4
HEAD_SIZE = 128
ADAPTER_SCALE = 2.0
PAD = 16
IDS = 128
VMEM_LIMIT = 60 * 1024 * 1024
BF16 = jnp.bfloat16
F32 = jnp.float32
ANY = pl.BlockSpec(memory_space=pl.ANY)
VMEM = pl.BlockSpec(memory_space=pltpu.VMEM)
SMEM = pl.BlockSpec(memory_space=pltpu.SMEM)


def call(body, out_shape, in_specs, scratch, name, args, cost=None):
    return pl.pallas_call(
        body,
        out_shape=out_shape,
        in_specs=in_specs,
        out_specs=[VMEM] * len(out_shape),
        scratch_shapes=scratch,
        compiler_params=pltpu.CompilerParams(vmem_limit_bytes=VMEM_LIMIT),
        cost_estimate=cost,
        name=name,
    )(*args)


def down_rows(lane_row):
    return jnp.broadcast_to(lane_row, (128, lane_row.shape[1])).T


def attend(q_of, own, idx, lens, pool_ref, kt_ref, vx_ref, bias_ref, s_ref, heads, store):
    rows = own.shape[0]
    D = HEAD_SIZE
    nblk, bs, _ = pool_ref.shape
    npos = nblk * bs
    nslot = idx.shape[0]
    scale = math.log2(math.e) / math.sqrt(D)
    pool = pool_ref[...].reshape(npos, 2 * D)
    kt_ref[...] = pool[:, :D].T
    vx_ref[:, :D] = pool[:, D:]
    vx_ref[:, D:] = jnp.ones((npos, D), BF16)
    nfull = jnp.floor(lens * (1.0 / bs))
    rem = lens - nfull * bs
    block = lax.broadcasted_iota(jnp.int32, (nblk, rows), 0).astype(F32)
    full = jnp.zeros((nblk, rows), F32)
    some = jnp.zeros((nblk, rows), F32)
    for j in range(nslot):
        hit = idx[j : j + 1, :] == block
        full += jnp.where(hit & (nfull > j), 1.0, 0.0)
        some += jnp.where(hit & (lens > j * bs), 1.0, 0.0)
    full = full.astype(BF16)
    some = some.astype(BF16)
    pad = -rows % 128
    rem_row = jnp.concatenate([rem, jnp.zeros((1, pad), F32)], 1) if pad else rem
    rem_col = down_rows(rem_row)[:rows]
    width = 512
    offset = (lax.broadcasted_iota(jnp.int32, (rows, 128), 1) % bs).astype(F32)
    partial = jnp.concatenate([offset < rem_col] * (width // 128), 1)
    over_rows = (((0,), (0,)), ((), ()))
    for w in range(0, npos, width):
        spot = lax.broadcasted_iota(jnp.int32, (nblk, width), 1) + w
        here = spot // bs == lax.broadcasted_iota(jnp.int32, (nblk, width), 0)
        spread = jnp.where(here, 1.0, 0.0).astype(BF16)
        count_full = lax.dot_general(full, spread, over_rows, preferred_element_type=F32)
        count_some = lax.dot_general(some, spread, over_rows, preferred_element_type=F32)
        count = jnp.where(partial, count_some, count_full)
        bias_ref[:, w : w + width] = jnp.where(
            count > 0.5, jnp.log2(jnp.maximum(count, 1.0)), -jnp.inf
        )
    own = own.astype(F32)
    own_k, own_v = own[:, :D], own[:, D:]
    for h in range(heads):
        q = q_of(h)
        top = None
        for w in range(0, npos, width):
            s = jnp.dot(q, kt_ref[:, w : w + width], preferred_element_type=F32)
            s = s * scale + bias_ref[:, w : w + width]
            s_ref[h % 2, :, w : w + width] = s
            for lane in range(0, width, 128):
                part = s[:, lane : lane + 128]
                top = part if top is None else jnp.maximum(top, part)
        own_s = jnp.sum(q.astype(F32) * own_k, axis=1, keepdims=True) * scale
        m = jnp.maximum(jnp.max(top, axis=1, keepdims=True), own_s)
        acc = jnp.zeros((rows, 2 * D), F32)
        for w in range(0, npos, width):
            p = jnp.exp2(s_ref[h % 2, :, w : w + width] - m).astype(BF16)
            acc += jnp.dot(p, vx_ref[w : w + width, :], preferred_element_type=F32)
        own_w = jnp.exp2(own_s - m)
        out = (acc[:, :D] + own_w * own_v) / (acc[:, D : D + 1] + own_w)
        store(h, out.astype(BF16))


def weight_copies(w_ref, held, sems, blocks):
    width = held.shape[2]
    out = []
    for i, block in enumerate(blocks):
        start = pl.multiple_of(block * width, width)
        out.append(pltpu.make_async_copy(w_ref.at[:, pl.ds(start, width)], held.at[i], sems.at[i]))
    return out


def chip_blocks(t, chips):
    chip, core = t // 2, t % 2
    out = []
    for d in range(1, chips):
        at = 2 * lax.rem(chip + d, chips)
        out += [at + 1 - core, at + core]
    return out


def first_kernel(n1, chips, members, sc_ref, leave_ref, recv_ref, q_ref, fresh_ref, idx_ref, len_ref, id_ref,
                 pool_ref, w_ref, attn_ref, send_ref, keep_ref, *rest):
    pays = rest[:members]
    pool, own_all, kt, vx, bias, s, aug_q, held, psem, wsem = rest[members:]
    t, z, kv = sc_ref[0], sc_ref[1], sc_ref[2]
    D = HEAD_SIZE
    kv_at = pl.multiple_of(kv * 2 * D, 2 * D)
    pool_copy = pltpu.make_async_copy(pool_ref.at[:, :, pl.ds(kv_at, 2 * D)], pool, psem.at[0])
    own_copy = pltpu.make_async_copy(fresh_ref.at[:, pl.ds(kv_at, 2 * D)], own_all, psem.at[1])
    own_copy.start()
    pool_copy.start()
    copies = weight_copies(w_ref, held, wsem, chip_blocks(t, chips))
    for c in copies:
        c.start()
    rows, channels = q_ref.shape
    moved = leave_ref.shape[1]
    heads = channels // D
    lane = lax.broadcasted_iota(jnp.int32, (PAD, rows), 1)
    row = lax.broadcasted_iota(jnp.int32, (PAD, rows), 0)
    pick = jnp.zeros((PAD, rows), jnp.bool_)
    for j in range(moved):
        pick = pick | ((row == j) & (lane == leave_ref[0, j]))
    pick = jnp.where(pick, 1.0, 0.0).astype(BF16)
    aug_q[:n1, :] = q_ref[:n1, :]
    aug_q[n1:, :] = jnp.dot(pick, q_ref[...], preferred_element_type=F32).astype(BF16)
    idx = idx_ref[...].astype(F32)
    lens = len_ref[...].astype(F32)
    ids = id_ref[...].astype(F32)
    both = jnp.concatenate([idx, jnp.broadcast_to(lens, (8, rows)), jnp.broadcast_to(ids, (8, rows))], 0)
    nt = (((1,), (1,)), ((), ()))
    out_of = lax.dot_general(both.astype(BF16), pick, nt, preferred_element_type=F32)
    ns = idx.shape[0]
    idx = jnp.concatenate([idx[:, :n1], out_of[:ns]], 1)
    lens = jnp.concatenate([lens[:, :n1], out_of[ns : ns + 1]], 1)
    id_col = lax.dot_general(pick, jnp.broadcast_to(ids, (128, rows)).astype(BF16), nt, preferred_element_type=F32)
    own_copy.wait()
    own = jnp.concatenate(
        [own_all[:n1, :], jnp.dot(pick, own_all[...], preferred_element_type=F32).astype(BF16)], 0
    )
    pool_copy.wait()
    left = []

    def store(h, out):
        attn_ref[:, h * D : (h + 1) * D] = out[:n1]
        left.append(out[n1:])

    attend(lambda h: aug_q[:, h * D : (h + 1) * D], own, idx, lens, pool, kt, vx, bias, s, heads, store)
    width = held.shape[2]
    a = attn_ref[...]
    for i, c in enumerate(copies):
        c.wait()
        ref = (send_ref, keep_ref)[i % 2]
        at = (i // 2) * width
        ref[:, at : at + width] = jnp.dot(a, held[i], preferred_element_type=F32).astype(BF16)
    left = jnp.concatenate(left + [id_col[:, :IDS].astype(BF16)], 1)
    mask_row = lax.broadcasted_iota(jnp.int32, left.shape, 0) < moved
    for k in range(members):
        mine = recv_ref[0] == lax.rem(z + k, members)
        pays[k][...] = jnp.where(mask_row & mine, left, jnp.zeros_like(left))


def second_kernel(n1, sc_ref, q_ref, fresh_ref, idx_ref, len_ref, pool_ref, attn_ref,
                  pool, own_all, kt, vx, bias, s, psem):
    kv = sc_ref[2]
    D = HEAD_SIZE
    kv_at = pl.multiple_of(kv * 2 * D, 2 * D)
    pool_copy = pltpu.make_async_copy(pool_ref.at[:, :, pl.ds(kv_at, 2 * D)], pool, psem.at[0])
    own_copy = pltpu.make_async_copy(fresh_ref.at[:, pl.ds(kv_at, 2 * D)], own_all, psem.at[1])
    own_copy.start()
    pool_copy.start()
    heads = q_ref.shape[1] // D
    own_copy.wait()
    pool_copy.wait()

    def store(h, out):
        attn_ref[:, h * D : (h + 1) * D] = out

    attend(lambda h: q_ref[n1:, h * D : (h + 1) * D], own_all[n1:, :], idx_ref[:, n1:].astype(F32),
           len_ref[:, n1:].astype(F32), pool, kt, vx, bias, s, heads, store)


def project_kernel(chips, members, sc_ref, attn_ref, w_ref, *rest):
    pays, (full_ref, arr_ref, send_ref, keep_ref, held, wsem) = rest[:members], rest[members:]
    copies = weight_copies(w_ref, held, wsem, chip_blocks(sc_ref[0], chips))
    for c in copies:
        c.start()
    arr = pays[0][...]
    for p in pays[1:]:
        arr = arr + p[...]
    arr_ref[...] = arr
    n, channels = attn_ref.shape
    full_ref[:n, :] = attn_ref[...]
    full_ref[n:, :] = arr[:, :channels]
    width = held.shape[2]
    a = full_ref[...]
    for i, c in enumerate(copies):
        c.wait()
        ref = (send_ref, keep_ref)[i % 2]
        at = (i // 2) * width
        ref[:, at : at + width] = jnp.dot(a, held[i], preferred_element_type=F32).astype(BF16)


def own_kernel(sc_ref, a1_ref, a2_ref, w_ref, send_ref, own_ref, held, wsem):
    t = sc_ref[0]
    core = t % 2
    copies = weight_copies(w_ref, held, wsem, [t + 1 - 2 * core, t])
    for c in copies:
        c.start()
    n1 = a1_ref.shape[0]
    for i, (c, ref) in enumerate(zip(copies, (send_ref, own_ref))):
        c.wait()
        for a, rows in ((a1_ref, slice(0, n1)), (a2_ref, slice(n1, None))):
            ref[rows, :] = jnp.dot(a[...], held[i], preferred_element_type=F32).astype(ref.dtype)


def shrink_kernel(members, groups, sc_ref, slots_ref, a1_ref, a2_ref, id_ref, arr_ref, own_down, *rest):
    same, swapped = rest[: members - 1], rest[members - 1 : 2 * (members - 1)]
    shr_ref, slot_ref = rest[2 * (members - 1) :]
    z, y = sc_ref[1], sc_ref[3]
    n1, channels = a1_ref.shape
    ids = down_rows(id_ref[...].astype(F32))
    ids = jnp.concatenate([ids, jnp.broadcast_to(arr_ref[:, channels : channels + 1].astype(F32), (PAD, 128))], 0)
    slot = jnp.zeros_like(ids)
    for a in range(slots_ref.shape[0]):
        slot = jnp.where(ids == a, slots_ref[a].astype(F32), slot)
    slot_ref[...] = slot
    nt = (((1,), (1,)), ((), ()))
    pieces = [(own_down[g], z * groups + g) for g in range(groups)]
    for k in range(1, members):
        layer = lax.rem(z + members - k, members) * groups
        pieces.append((same[k - 1][...], layer + y))
        pieces.append((swapped[k - 1][...], layer + 1 - y))
    rank = own_down.shape[1]
    for a, lo, hi in ((a1_ref, 0, n1), (a2_ref, n1, slot.shape[0])):
        total = jnp.zeros((hi - lo, 2 * rank), F32)
        for i in range(0, len(pieces), 2):
            table = jnp.concatenate([pieces[i][0], pieces[i + 1][0]], 0)
            part = lax.dot_general(a[...], table, nt, preferred_element_type=F32)
            left = lax.broadcasted_iota(jnp.int32, part.shape, 1) < rank
            at = jnp.where(left, pieces[i][1].astype(F32), pieces[i + 1][1].astype(F32))
            total += jnp.where(slot[lo:hi, : 2 * rank] == at, part, 0.0)
        shr_ref[lo:hi, :] = total[:, :rank] + total[:, rank:]


def final_kernel(members, groups, chips, sc_ref, leave_ref, shr_ref, slot_ref, own_ref, recv_ref, own_up, *rest):
    same, swapped = rest[: members - 1], rest[members - 1 : 2 * (members - 1)]
    rest = rest[2 * (members - 1) :]
    shr_in, rest = rest[: chips - 1], rest[chips - 1 :]
    x1, x2 = rest[: chips - 1], rest[chips - 1 : 2 * (chips - 1)]
    out_ref = rest[2 * (chips - 1)]
    z, y = sc_ref[1], sc_ref[3]
    shrunk = shr_ref[...]
    for r in shr_in:
        shrunk = shrunk + r[...].astype(F32)
    shrunk = shrunk.astype(BF16).astype(F32)
    rank = own_up.shape[1]
    wide = jnp.concatenate([shrunk, shrunk], 1)
    slot = slot_ref[:, : 2 * rank]
    pieces = [(own_up[g], z * groups + g) for g in range(groups)]
    for k in range(1, members):
        layer = lax.rem(z + members - k, members) * groups
        pieces.append((same[k - 1][...], layer + y))
        pieces.append((swapped[k - 1][...], layer + 1 - y))
    left = lax.broadcasted_iota(jnp.int32, wide.shape, 1) < rank
    delta = None
    for i in range(0, len(pieces), 2):
        at = jnp.where(left, pieces[i][1].astype(F32), pieces[i + 1][1].astype(F32))
        spread = jnp.where(slot == at, wide, 0.0).astype(BF16)
        table = jnp.concatenate([pieces[i][0], pieces[i + 1][0]], 0)
        part = jnp.dot(spread, table, preferred_element_type=F32)
        delta = part if delta is None else delta + part
    base = own_ref[...] + recv_ref[...].astype(F32)
    for a, b in zip(x1, x2):
        base = base + jnp.concatenate([a[...], b[...]], 0).astype(F32)
    result = base + ADAPTER_SCALE * delta
    rows = out_ref.shape[0]
    moved = leave_ref.shape[1]
    row = lax.broadcasted_iota(jnp.int32, out_ref.shape, 0)
    out = result[:rows]
    for j in range(moved):
        out = jnp.where(row == leave_ref[0, j], result[rows + j : rows + j + 1], out)
    out_ref[...] = out.astype(BF16)


def add_kernel(a_ref, b_ref, o_ref):
    o_ref[...] = (a_ref[...].astype(F32) + b_ref[...].astype(F32)).astype(o_ref.dtype)


def after(value, *others):
    return lax.optimization_barrier((value,) + others)[0]


def on_device(mesh_shape, queries, fresh, pool, table, lengths, adapter_id, storage_slot, leaving, receiving,
              w, down, up):
    members, tensors, groups = mesh_shape["replica"], mesh_shape["tensor"], mesh_shape["groups"]
    chips = tensors // 2
    rows, channels = queries.shape
    heads = channels // HEAD_SIZE
    nblk, bs, _ = pool.shape
    npos = nblk * bs
    cols = w.shape[1] // tensors
    rank = down.shape[2]
    n1 = rows // 2
    n2 = rows - n1
    t = lax.axis_index("tensor")
    z = lax.axis_index("replica")
    y = lax.axis_index("groups")
    kv = t * heads // (QUERY_HEADS_HALF // KVH)
    sc = jnp.stack([t, z, kv, y]).astype(jnp.int32)
    idx_t = table.T
    len_row = lengths[None, :]
    id_row = adapter_id[None, :]
    down_t = jnp.swapaxes(down, 1, 2)

    def shift(v, k):
        return lax.ppermute(v, "replica", [(i, (i + k) % members) for i in range(members)])

    def swap(v):
        return lax.ppermute(v, "groups", [(0, 1), (1, 0)])

    def core(v):
        return lax.ppermute(v, "tensor", [(i, i ^ 1) for i in range(tensors)])

    def chip(v, d):
        return lax.ppermute(v, "tensor", [(i, (i + 2 * d) % tensors) for i in range(tensors)])

    mine_down = lax.dynamic_index_in_dim(down_t, y, 0, keepdims=False)
    mine_up = lax.dynamic_index_in_dim(up, y, 0, keepdims=False)
    down_same = [shift(mine_down, k) for k in range(1, members)]

    sds = jax.ShapeDtypeStruct
    dma = pltpu.SemaphoreType.DMA
    far = (chips - 1) * cols
    aug = n1 + PAD
    attn_scratch = lambda n: [
        pltpu.VMEM((HEAD_SIZE, npos), BF16),
        pltpu.VMEM((npos, 2 * HEAD_SIZE), BF16),
        pltpu.VMEM((n, npos), F32),
        pltpu.VMEM((2, n, npos), F32),
    ]
    pool_scratch = [pltpu.VMEM((nblk, bs, 2 * HEAD_SIZE), BF16), pltpu.VMEM((rows, 2 * HEAD_SIZE), BF16)]
    far_scratch = [pltpu.VMEM((2 * (chips - 1), channels, cols), BF16)]
    out1 = call(
        functools.partial(first_kernel, n1, chips, members),
        [sds((n1, channels), BF16), sds((n1, far), BF16), sds((n1, far), BF16)]
        + [sds((PAD, channels + IDS), BF16)] * members,
        [SMEM, SMEM, SMEM, VMEM, ANY, VMEM, VMEM, VMEM, ANY, ANY],
        pool_scratch + attn_scratch(aug) + [pltpu.VMEM((aug, channels), BF16)] + far_scratch
        + [dma((2,)), dma((2 * (chips - 1),))],
        "attend_and_project_first_rows",
        (sc, leaving, receiving, queries, fresh, idx_t, len_row, id_row, pool, w),
    )
    attn1, send1, keep1 = out1[:3]
    pays = out1[3:]

    def reduce_far(send, keep):
        got = core(send)
        total = call(add_kernel, [sds(keep.shape, BF16)], [VMEM, VMEM], [], "add_partner_core", (keep, got))[0]
        return [chip(total[:, (d - 1) * cols : d * cols] if chips > 2 else total, d) for d in range(1, chips)]

    x1 = reduce_far(send1, keep1)
    arrived = [pays[0]] + [shift(pays[k], k) for k in range(1, members)]
    up_from = after(mine_up, attn1)
    up_same = [shift(up_from, k) for k in range(1, members)]
    down_swapped = [swap(v) for v in down_same]

    (attn2,) = call(
        functools.partial(second_kernel, n1),
        [sds((n2, channels), BF16)],
        [SMEM, VMEM, ANY, VMEM, VMEM, ANY],
        pool_scratch + attn_scratch(n2) + [dma((2,))],
        "attend_second_rows",
        (sc, after(queries, attn1), fresh, idx_t, len_row, pool),
    )
    full2, arr, send2, keep2 = call(
        functools.partial(project_kernel, chips, members),
        [sds((n2 + PAD, channels), BF16), sds((PAD, channels + IDS), BF16), sds((n2 + PAD, far), BF16),
         sds((n2 + PAD, far), BF16)],
        [SMEM, VMEM, ANY] + [VMEM] * members,
        far_scratch + [dma((2 * (chips - 1),))],
        "project_second_rows",
        (sc, attn2, w, *arrived),
    )
    x2 = reduce_far(send2, keep2)
    total_rows = rows + PAD
    send3, own = call(
        own_kernel,
        [sds((total_rows, cols), BF16), sds((total_rows, cols), F32)],
        [SMEM, VMEM, VMEM, ANY],
        [pltpu.VMEM((2, channels, cols), BF16), dma((2,))],
        "project_own_columns",
        (sc, attn1, after(full2, send2), w),
    )
    recv3 = core(send3)
    shr, slot = call(
        functools.partial(shrink_kernel, members, groups),
        [sds((total_rows, rank), F32), sds((total_rows, 128), F32)],
        [SMEM, SMEM, VMEM, VMEM, VMEM, VMEM, VMEM] + [VMEM] * (2 * (members - 1)),
        [],
        "shrink",
        (sc, storage_slot, attn1, full2, id_row, arr, down_t, *down_same, *down_swapped),
    )
    shr = shr + core(shr)
    shr16 = shr.astype(BF16)
    shr_in = [chip(shr16, d) for d in range(1, chips)]
    up_swapped = [swap(v) for v in up_same]

    tile = min(cols, 512)
    col = lambda n: pl.BlockSpec((n, tile), lambda i: (0, i))
    fixed = lambda *shape: pl.BlockSpec(shape, lambda i: (0,) * len(shape))
    return pl.pallas_call(
        functools.partial(final_kernel, members, groups, chips),
        grid=(cols // tile,),
        out_shape=sds((rows, cols), BF16),
        in_specs=[SMEM, SMEM, fixed(total_rows, rank), fixed(total_rows, 128), col(total_rows), col(total_rows),
                  pl.BlockSpec((groups, rank, tile), lambda i: (0, 0, i))]
        + [col(rank)] * (2 * (members - 1)) + [fixed(total_rows, rank)] * (chips - 1)
        + [col(n1)] * (chips - 1) + [col(n2 + PAD)] * (chips - 1),
        out_specs=col(rows),
        compiler_params=pltpu.CompilerParams(vmem_limit_bytes=VMEM_LIMIT),
        name="combine",
    )(sc, leaving, shr, slot, own, recv3, up, *up_same, *up_swapped, *shr_in, *x1, *x2)


def solution(mesh):
    return jax.shard_map(
        functools.partial(on_device, dict(mesh.shape)),
        mesh=mesh,
        in_specs=(
            P(("groups", "replica"), "tensor"),
            P(("groups", "replica"), None),
            P(("groups", "replica"), None, None),
            P(("groups", "replica"), None),
            P(("groups", "replica")),
            P(("groups", "replica")),
            P(),
            P(("groups", "replica"), None),
            P(("groups", "replica")),
            P("tensor", None),
            P("replica", "tensor", None),
            P("replica", None, "tensor"),
        ),
        out_specs=P(("groups", "replica"), "tensor"),
        check_vma=False,
    )
```

```python
import functools
import math

import jax
import jax.numpy as jnp
from jax import lax
from jax.experimental import pallas as pl
from jax.experimental.pallas import tpu as pltpu
from jax.sharding import PartitionSpec as P

QUERY_HEADS_HALF = 32
KVH = 4
HEAD_SIZE = 128
ADAPTER_SCALE = 2.0
RUNS = (5, 5, 6)
LONG = 200
PAD = 16
IDS = 128
VMEM_LIMIT = 60 * 1024 * 1024
BF16 = jnp.bfloat16
F32 = jnp.float32
ANY = pl.BlockSpec(memory_space=pl.ANY)
VMEM = pl.BlockSpec(memory_space=pltpu.VMEM)
SMEM = pl.BlockSpec(memory_space=pltpu.SMEM)


def cost(micros):
    return pl.CostEstimate(flops=int(micros * 1.15e9), bytes_accessed=1024, transcendentals=0)


def call(body, out_shape, in_specs, scratch, name, args, micros, limit=VMEM_LIMIT):
    return pl.pallas_call(
        body,
        out_shape=out_shape,
        in_specs=in_specs,
        out_specs=[VMEM] * len(out_shape),
        scratch_shapes=scratch,
        compiler_params=pltpu.CompilerParams(vmem_limit_bytes=limit),
        cost_estimate=cost(micros),
        name=name,
    )(*args)


def down_rows(lane_row):
    return jnp.broadcast_to(lane_row, (128, lane_row.shape[1])).T


def attend(q_of, own_of, idx, lens, pool_ref, at, k_ref, v_ref, sems, bias_ref, s_ref, heads, store):
    rows = idx.shape[1]
    D = HEAD_SIZE
    nblk, bs, _ = pool_ref.shape
    npos = nblk * bs
    scale = math.log2(math.e) / math.sqrt(D)
    k_copy = pltpu.make_async_copy(pool_ref.at[:, :, pl.ds(at, D)], k_ref, sems.at[0])
    v_copy = pltpu.make_async_copy(
        pool_ref.at[:, :, pl.ds(pl.multiple_of(at + D, D), D)], v_ref.at[:, :, pl.ds(0, D)], sems.at[1]
    )
    k_copy.start()
    v_copy.start()
    v_ref[:, :, D:] = jnp.ones((nblk, bs, D), BF16)
    nfull = jnp.floor(lens * (1.0 / bs))
    rem = lens - nfull * bs
    block = lax.broadcasted_iota(jnp.int32, (nblk, rows), 0).astype(F32)
    full = jnp.zeros((nblk, rows), F32)
    some = jnp.zeros((nblk, rows), F32)
    for j in range(idx.shape[0]):
        hit = idx[j : j + 1, :] == block
        full += jnp.where(hit & (nfull > j), 1.0, 0.0)
        some += jnp.where(hit & (lens > j * bs), 1.0, 0.0)
    full = full.astype(BF16)
    some = some.astype(BF16)
    width = 512
    offset = (lax.broadcasted_iota(jnp.int32, (rows, 128), 1) % bs).astype(F32)
    partial = jnp.concatenate([offset < down_rows(rem)] * (width // 128), 1)
    over_rows = (((0,), (0,)), ((), ()))
    for w in range(0, npos, width):
        spot = lax.broadcasted_iota(jnp.int32, (nblk, width), 1) + w
        here = spot // bs == lax.broadcasted_iota(jnp.int32, (nblk, width), 0)
        spread = jnp.where(here, 1.0, 0.0).astype(BF16)
        count_full = lax.dot_general(full, spread, over_rows, preferred_element_type=F32)
        count_some = lax.dot_general(some, spread, over_rows, preferred_element_type=F32)
        count = jnp.where(partial, count_some, count_full)
        bias_ref[:, w : w + width] = jnp.where(
            count > 0.5, jnp.log2(jnp.maximum(count, 1.0)), -jnp.inf
        )
    own = own_of().astype(F32)
    own_k, own_v = own[:, :D], own[:, D:]
    k_copy.wait()
    v_copy.wait()
    keys = k_ref[...].reshape(npos, D)
    values = v_ref[...].reshape(npos, 2 * D)
    nt = (((1,), (1,)), ((), ()))
    before = None
    width = 1024
    for h in range(heads + 1):
        top = acc = None
        for w in range(0, npos, width):
            if h < heads:
                s = lax.dot_general(q_of(h), keys[w : w + width], nt, preferred_element_type=F32)
                s = s * scale + bias_ref[:, w : w + width]
                s_ref[h % 2, :, w : w + width] = s
                for lane in range(0, width, 128):
                    part = s[:, lane : lane + 128]
                    top = part if top is None else jnp.maximum(top, part)
            if h:
                p = jnp.exp2(s_ref[(h - 1) % 2, :, w : w + width] - before[1]).astype(BF16)
                part = jnp.dot(p, values[w : w + width], preferred_element_type=F32)
                acc = part if acc is None else acc + part
        if h:
            own_w = jnp.exp2(before[0] - before[1])
            out = (acc[:, :D] + own_w * own_v) / (acc[:, D : D + 1] + own_w)
            store(h - 1, out.astype(BF16))
        if h < heads:
            own_s = jnp.sum(q_of(h).astype(F32) * own_k, axis=1, keepdims=True) * scale
            before = own_s, jnp.maximum(jnp.max(top, axis=1, keepdims=True), own_s)


def weight_copies(w_ref, held, sems, blocks):
    width = held.shape[2]
    out = []
    for i, block in enumerate(blocks):
        start = pl.multiple_of(block * width, width)
        out.append(pltpu.make_async_copy(w_ref.at[:, pl.ds(start, width)], held.at[i], sems.at[i]))
    return out


def chip_blocks(t, chips):
    chip, core = t // 2, t % 2
    out = []
    for d in range(1, chips):
        at = 2 * lax.rem(chip + d, chips)
        out += [at + 1 - core, at + core]
    return out


def attend_kernel(chips, members, sc_ref, leave_ref, recv_ref, q_ref, fresh_ref, idx_ref, len_ref, id_ref, pool_ref,
                  w_ref, attn_ref, *rest):
    sends, keeps, rest = rest[: len(RUNS)], rest[len(RUNS) : 2 * len(RUNS)], rest[2 * len(RUNS) :]
    pays, (k_ref, v_ref, fresh, bias, s, held, psem, wsem) = rest[:members], rest[members:]
    t, z, kv = sc_ref[0], sc_ref[1], sc_ref[2]
    D = HEAD_SIZE
    rows, channels = attn_ref.shape
    at = pl.multiple_of(kv * 2 * D, 2 * D)
    own_copy = pltpu.make_async_copy(fresh_ref.at[:, pl.ds(at, 2 * D)], fresh, psem.at[2])
    own_copy.start()
    copies = weight_copies(w_ref, held, wsem, chip_blocks(t, chips))

    def own_of():
        for c in copies:
            c.start()
        own_copy.wait()
        return fresh[...]

    def store(h, out):
        attn_ref[:, h * D : (h + 1) * D] = out

    attend(lambda h: q_ref[:, h * D : (h + 1) * D], own_of, idx_ref[...].astype(F32),
           len_ref[...].astype(F32), pool_ref, at, k_ref, v_ref, psem, bias, s, channels // D, store)
    a = attn_ref[...]
    width = held.shape[2]
    for i, c in enumerate(copies):
        c.wait()
        lo = (i // 2) * width
        out = jnp.dot(a, held[i], preferred_element_type=F32).astype(BF16)
        row = 0
        for ref in (sends, keeps)[i % 2]:
            ref[:, lo : lo + width] = out[row : row + ref.shape[0]]
            row += ref.shape[0]
    moved = leave_ref.shape[1]
    lane = lax.broadcasted_iota(jnp.int32, (PAD, rows), 1)
    row = lax.broadcasted_iota(jnp.int32, (PAD, rows), 0)
    pick = jnp.zeros((PAD, rows), jnp.bool_)
    for j in range(moved):
        pick = pick | ((row == j) & (lane == leave_ref[0, j]))
    pick = jnp.where(pick, 1.0, 0.0).astype(BF16)
    left = jnp.dot(pick, a, preferred_element_type=F32)
    nt = (((1,), (1,)), ((), ()))
    ids = jnp.broadcast_to(id_ref[...].astype(F32), (IDS, rows)).astype(BF16)
    id_col = lax.dot_general(pick, ids, nt, preferred_element_type=F32)
    left = jnp.concatenate([left, id_col], 1).astype(BF16)
    for k in range(members):
        pays[k][...] = jnp.where(recv_ref[0] == (z ^ k), left, jnp.zeros_like(left))


def own_kernel(members, sc_ref, slots_ref, leave_ref, w_ref, id_ref, attn_ref, *rest):
    pays, (send_ref, own_ref, fixed, slot_ref, arr_ref, held, wsem) = rest[:members], rest[members:]
    t = sc_ref[0]
    copies = weight_copies(w_ref, held, wsem, [t + 1 - 2 * (t % 2), t])
    for c in copies:
        c.start()
    rows, channels = fixed.shape
    moved = leave_ref.shape[1]
    arr = pays[0][...]
    for p in pays[1:]:
        arr = arr + p[...]
    arr_ref[...] = arr[:, :channels]
    row = lax.broadcasted_iota(jnp.int32, (rows, channels), 0)
    whole = attn_ref[...].astype(F32)
    for j in range(moved):
        whole = jnp.where(row == leave_ref[0, j], arr[j : j + 1, :channels].astype(F32), whole)
    fixed[...] = whole.astype(BF16)
    ids = down_rows(id_ref[...].astype(F32))
    came = arr[:, channels:].astype(F32)
    row = lax.broadcasted_iota(jnp.int32, ids.shape, 0)
    for j in range(moved):
        ids = jnp.where(row == leave_ref[0, j], came[j : j + 1, 0:1], ids)
    slot = jnp.zeros_like(ids)
    for i in range(slots_ref.shape[0]):
        slot = jnp.where(ids == i, slots_ref[i].astype(F32), slot)
    slot_ref[...] = slot
    a = fixed[...]
    for i, (c, ref) in enumerate(zip(copies, (send_ref, own_ref))):
        c.wait()
        ref[...] = jnp.dot(a, held[i], preferred_element_type=F32).astype(BF16)


def shrink_kernel(members, groups, chips, sc_ref, w_ref, attn_ref, slot_ref, arr_ref, own_down, *rest):
    same, swapped, rest = rest[: members - 1], rest[members - 1 : 2 * (members - 1)], rest[2 * (members - 1) :]
    pack_send, pack_keep, held, wsem = rest
    t, z, y = sc_ref[0], sc_ref[1], sc_ref[3]
    copies = weight_copies(w_ref, held, wsem, chip_blocks(t, chips))
    for c in copies:
        c.start()
    rows, channels = attn_ref.shape
    a = attn_ref[...]
    rank = own_down.shape[1]
    nt = (((1,), (1,)), ((), ()))
    slot = slot_ref[:, : 2 * rank]
    total = jnp.zeros((rows, 2 * rank), F32)
    left = lax.broadcasted_iota(jnp.int32, total.shape, 1) < rank
    pieces = slot_pieces(members, groups, z, y, own_down, same, swapped)
    for (one, one_at), (two, two_at) in zip(pieces[::2], pieces[1::2]):
        part = lax.dot_general(a, jnp.concatenate([one, two], 0), nt, preferred_element_type=F32)
        total += jnp.where(slot == jnp.where(left, one_at, two_at).astype(F32), part, 0.0)
    shr = total[:, :rank] + total[:, rank:]
    shr = jnp.concatenate([shr, jnp.zeros((rows, 128 - rank), F32)], 1).astype(BF16)
    arr = arr_ref[...]
    width = held.shape[2]
    for i, c in enumerate(copies):
        c.wait()
        pack = (pack_send, pack_keep)[i % 2]
        out = jnp.dot(arr, held[i], preferred_element_type=F32).astype(BF16)
        parts = [out[:, c : c + 128] for c in range(0, width, 128)]
        lo, size = (i // 2) * rows, PAD * len(parts)
        pack[lo : lo + size, :128] = jnp.concatenate(parts, 0)
        if size < rows:
            pack[lo + size : lo + rows, :128] = jnp.zeros((rows - size, 128), BF16)
        pack[lo : lo + rows, 128:] = shr


def slot_pieces(members, groups, z, y, own, same, swapped):
    pieces = [(own[g], z * groups + g) for g in range(groups)]
    for k in range(1, members):
        layer = (z ^ k) * groups
        pieces.append((same[k - 1][...], layer + y))
        pieces.append((swapped[k - 1][...], layer + 1 - y))
    return pieces


def final_kernel(members, groups, chips, sc_ref, leave_ref, slot_ref, own_ref, got_ref, own_up, *rest):
    same, swapped = rest[: members - 1], rest[members - 1 : 2 * (members - 1)]
    rest = rest[2 * (members - 1) :]
    packs, rest = rest[:chips], rest[chips:]
    moves, far, out_ref = rest[: chips - 1], rest[chips - 1 : -1], rest[-1]
    z, y = sc_ref[1], sc_ref[3]
    rank = own_up.shape[1]
    shrunk = sum(p[:, 128 : 128 + rank].astype(F32) for p in packs)
    shrunk = shrunk.astype(BF16).astype(F32)
    wide = jnp.concatenate([shrunk, shrunk], 1)
    slot = slot_ref[:, : 2 * rank]
    left = lax.broadcasted_iota(jnp.int32, wide.shape, 1) < rank
    delta = None
    pieces = slot_pieces(members, groups, z, y, own_up, same, swapped)
    for (one, one_at), (two, two_at) in zip(pieces[::2], pieces[1::2]):
        spread = jnp.where(slot == jnp.where(left, one_at, two_at).astype(F32), wide, 0.0).astype(BF16)
        part = jnp.dot(spread, jnp.concatenate([one, two], 0), preferred_element_type=F32)
        delta = part if delta is None else delta + part
    base = own_ref[...].astype(F32) + got_ref[...].astype(F32) + ADAPTER_SCALE * delta
    others = jnp.concatenate(
        [sum(r[...].astype(F32) for r in far[i : i + chips - 1]) for i in range(0, len(far), chips - 1)], 0
    )
    came = sum(r[...].astype(F32) for r in moves)
    row = lax.broadcasted_iota(jnp.int32, base.shape, 0)
    for j in range(leave_ref.shape[1]):
        new = jnp.concatenate([came[c + j : c + j + 1, :] for c in range(0, came.shape[0], PAD)], 1)
        others = jnp.where(row == leave_ref[0, j], new, others)
    out_ref[...] = (base + others).astype(BF16)


def after(value, *others):
    return lax.optimization_barrier((value,) + others)[0]


def on_device(mesh_shape, queries, fresh, pool, table, lengths, adapter_id, storage_slot, leaving, receiving,
              w, down, up):
    members, tensors, groups = mesh_shape["replica"], mesh_shape["tensor"], mesh_shape["groups"]
    chips = tensors // 2
    rows, channels = queries.shape
    heads = channels // HEAD_SIZE
    nblk, bs, _ = pool.shape
    npos = nblk * bs
    cols = w.shape[1] // tensors
    rank = down.shape[2]
    t = lax.axis_index("tensor")
    z = lax.axis_index("replica")
    y = lax.axis_index("groups")
    kv = t * heads // (QUERY_HEADS_HALF // KVH)
    sc = jnp.stack([t, z, kv, y]).astype(jnp.int32)
    idx_t = table.T
    len_row = lengths[None, :]
    id_row = adapter_id[None, :]
    down_t = jnp.swapaxes(down, 1, 2)

    def across(v, k):
        return lax.ppermute(v, "replica", [(i, i ^ k) for i in range(members)])

    def swap(v):
        return lax.ppermute(v, "groups", [(0, 1), (1, 0)])

    def core(v):
        return lax.ppermute(v, "tensor", [(i, i ^ 1) for i in range(tensors)])

    def chip(v, d):
        return lax.ppermute(v, "tensor", [(i, (i + 2 * d) % tensors) for i in range(tensors)])

    def to_chips(v):
        return [chip(v[:, (d - 1) * cols : d * cols] if chips > 2 else v, d) for d in range(1, chips)]

    mine_down = lax.dynamic_index_in_dim(down_t, y, 0, keepdims=False)
    mine_up = lax.dynamic_index_in_dim(up, y, 0, keepdims=False)

    def near(v):
        return {1 << i: across(v, 1 << i) for i in reversed(range(members.bit_length() - 1))}

    def passed(v, have):
        have = {0: v, **have}
        bit = members // 2
        while bit:
            for k in [k for k in have if k % (2 * bit) == 0 and k ^ bit not in have]:
                have[k ^ bit] = across(have[k], bit)
            bit //= 2
        return [have[k] for k in range(1, members)]

    down_near = near(mine_down)
    up_near = near(mine_up)
    sds = jax.ShapeDtypeStruct
    dma = pltpu.SemaphoreType.DMA
    far = (chips - 1) * cols
    sizes = [rows * r // sum(RUNS) for r in RUNS]
    attn, *out = call(
        functools.partial(attend_kernel, chips, members),
        [sds((rows, channels), BF16)] + [sds((n, far), BF16) for n in sizes] * 2
        + [sds((PAD, channels + IDS), BF16)] * members,
        [SMEM, SMEM, SMEM, VMEM, ANY, VMEM, VMEM, VMEM, ANY, ANY],
        [
            pltpu.VMEM((nblk, bs, HEAD_SIZE), BF16),
            pltpu.VMEM((nblk, bs, 2 * HEAD_SIZE), BF16),
            pltpu.VMEM((rows, 2 * HEAD_SIZE), BF16),
            pltpu.VMEM((rows, npos), F32),
            pltpu.VMEM((2, rows, npos), F32),
            pltpu.VMEM((2 * (chips - 1), channels, cols), BF16),
            dma((3,)),
            dma((2 * (chips - 1),)),
        ],
        "attend_and_project",
        (sc, leaving, receiving, queries, fresh, idx_t, len_row, id_row, pool, w),
        LONG,
    )
    runs = len(RUNS)
    sends, keeps, pays = out[:runs], out[runs : 2 * runs], out[2 * runs :]
    sends[0] = after(sends[0], *down_near.values(), *up_near.values())
    totals = []
    for send, keep in zip(sends, keeps):
        totals.append(after(keep, *totals) + core(send))
    x_in = [to_chips(total) for total in totals]
    arrived = [pays[0]] + [across(pays[k], k) for k in range(1, members)]
    down_same = passed(after(mine_down, attn), down_near)
    up_same = passed(after(mine_up, attn), up_near)
    down_swapped = {k: swap(after(v, attn)) for k, v in down_near.items()}
    up_swapped = {k: swap(after(v, attn)) for k, v in up_near.items()}
    early = [*down_same, *down_swapped.values(), *x_in[0]]
    send_own, own, fixed, slot, arr = call(
        functools.partial(own_kernel, members),
        [sds((rows, cols), BF16), sds((rows, cols), BF16), sds((rows, channels), BF16), sds((rows, 128), F32),
         sds((PAD, channels), BF16)],
        [SMEM, SMEM, SMEM, ANY, VMEM, VMEM] + [VMEM] * members,
        [pltpu.VMEM((2, channels, cols), BF16), dma((2,))],
        "project_own_columns",
        (sc, storage_slot, leaving, w, id_row, after(attn, *early), *arrived),
        LONG,
    )
    got_own = core(send_own)
    for k in range(1, members):
        if k not in up_swapped:
            down_swapped[k] = swap(down_same[k - 1])
            up_swapped[k] = swap(up_same[k - 1])
    down_swapped = [down_swapped[k] for k in range(1, members)]
    up_swapped = [up_swapped[k] for k in range(1, members)]
    pack_send, pack_keep = call(
        functools.partial(shrink_kernel, members, groups, chips),
        [sds(((chips - 1) * rows, 256), BF16)] * 2,
        [SMEM, ANY] + [VMEM] * (4 + 2 * (members - 1)),
        [pltpu.VMEM((2 * (chips - 1), channels, cols), BF16), dma((2 * (chips - 1),))],
        "shrink_and_project_arrived",
        (sc, w, after(fixed, *up_same, up_swapped[members // 2 - 1], *x_in[1]), slot, arr, down_t, *down_same,
         *down_swapped),
        LONG,
    )
    pack = pack_keep + core(pack_send)
    packs = [pack[:rows]] + [chip(pack[(d - 1) * rows : d * rows], d) for d in range(1, chips)]

    tile = cols // 4
    col = lambda n: pl.BlockSpec((n, tile), lambda i: (0, i))
    still = lambda *shape: pl.BlockSpec(shape, lambda i: (0,) * len(shape))
    strip = pl.BlockSpec((PAD * tile // 128, 128), lambda i: (i, 0))
    return pl.pallas_call(
        functools.partial(final_kernel, members, groups, chips),
        grid=(cols // tile,),
        out_shape=sds((rows, cols), BF16),
        in_specs=[SMEM, SMEM, still(rows, 128), col(rows), col(rows),
                  pl.BlockSpec((groups, rank, tile), lambda i: (0, 0, i))]
        + [col(rank)] * (2 * (members - 1)) + [still(rows, 256)] * chips + [strip] * (chips - 1)
        + [col(n) for n in sizes for _ in range(chips - 1)],
        out_specs=col(rows),
        compiler_params=pltpu.CompilerParams(vmem_limit_bytes=VMEM_LIMIT),
        cost_estimate=cost(5),
        name="combine",
    )(sc, leaving, slot, own, got_own, up, *up_same, *up_swapped, *packs, *packs[1:], *[v for x in x_in for v in x])


def solution(mesh):
    return jax.shard_map(
        functools.partial(on_device, dict(mesh.shape)),
        mesh=mesh,
        in_specs=(
            P(("groups", "replica"), "tensor"),
            P(("groups", "replica"), None),
            P(("groups", "replica"), None, None),
            P(("groups", "replica"), None),
            P(("groups", "replica")),
            P(("groups", "replica")),
            P(),
            P(("groups", "replica"), None),
            P(("groups", "replica")),
            P("tensor", None),
            P("replica", "tensor", None),
            P("replica", None, "tensor"),
        ),
        out_specs=P(("groups", "replica"), "tensor"),
        check_vma=False,
    )
```

```python
import functools
import math

import jax
import jax.numpy as jnp
from jax import lax
from jax.experimental import pallas as pl
from jax.experimental.pallas import tpu as pltpu
from jax.sharding import PartitionSpec as P

QUERY_HEADS_HALF = 32
KVH = 4
HEAD_SIZE = 128
ADAPTER_SCALE = 2.0
RUNS = (1,)
LONG = 200
PAD = 16
IDS = 128
VMEM_LIMIT = 60 * 1024 * 1024
BF16 = jnp.bfloat16
F32 = jnp.float32
ANY = pl.BlockSpec(memory_space=pl.ANY)
VMEM = pl.BlockSpec(memory_space=pltpu.VMEM)
SMEM = pl.BlockSpec(memory_space=pltpu.SMEM)


def cost(micros):
    return pl.CostEstimate(flops=int(micros * 1.15e9), bytes_accessed=1024, transcendentals=0)


def call(body, out_shape, in_specs, scratch, name, args, micros, limit=VMEM_LIMIT):
    return pl.pallas_call(
        body,
        out_shape=out_shape,
        in_specs=in_specs,
        out_specs=[VMEM] * len(out_shape),
        scratch_shapes=scratch,
        compiler_params=pltpu.CompilerParams(vmem_limit_bytes=limit),
        cost_estimate=cost(micros),
        name=name,
    )(*args)


def down_rows(lane_row):
    return jnp.broadcast_to(lane_row, (128, lane_row.shape[1])).T


def attend(q_of, own_of, idx, lens, pool_ref, at, k_ref, v_ref, sems, bias_ref, s_ref, heads, store):
    rows = idx.shape[1]
    D = HEAD_SIZE
    nblk, bs, _ = pool_ref.shape
    npos = nblk * bs
    scale = math.log2(math.e) / math.sqrt(D)
    k_copy = pltpu.make_async_copy(pool_ref.at[:, :, pl.ds(at, D)], k_ref, sems.at[0])
    v_copy = pltpu.make_async_copy(
        pool_ref.at[:, :, pl.ds(pl.multiple_of(at + D, D), D)], v_ref.at[:, :, pl.ds(0, D)], sems.at[1]
    )
    k_copy.start()
    v_copy.start()
    v_ref[:, :, D:] = jnp.ones((nblk, bs, D), BF16)
    nfull = jnp.floor(lens * (1.0 / bs))
    rem = lens - nfull * bs
    block = lax.broadcasted_iota(jnp.int32, (nblk, rows), 0).astype(F32)
    full = jnp.zeros((nblk, rows), F32)
    some = jnp.zeros((nblk, rows), F32)
    for j in range(idx.shape[0]):
        hit = idx[j : j + 1, :] == block
        full += jnp.where(hit & (nfull > j), 1.0, 0.0)
        some += jnp.where(hit & (lens > j * bs), 1.0, 0.0)
    full = full.astype(BF16)
    some = some.astype(BF16)
    width = 512
    offset = (lax.broadcasted_iota(jnp.int32, (rows, 128), 1) % bs).astype(F32)
    partial = jnp.concatenate([offset < down_rows(rem)] * (width // 128), 1)
    over_rows = (((0,), (0,)), ((), ()))
    for w in range(0, npos, width):
        spot = lax.broadcasted_iota(jnp.int32, (nblk, width), 1) + w
        here = spot // bs == lax.broadcasted_iota(jnp.int32, (nblk, width), 0)
        spread = jnp.where(here, 1.0, 0.0).astype(BF16)
        count_full = lax.dot_general(full, spread, over_rows, preferred_element_type=F32)
        count_some = lax.dot_general(some, spread, over_rows, preferred_element_type=F32)
        count = jnp.where(partial, count_some, count_full)
        bias_ref[:, w : w + width] = jnp.where(
            count > 0.5, jnp.log2(jnp.maximum(count, 1.0)), -jnp.inf
        )
    own = own_of().astype(F32)
    own_k, own_v = own[:, :D], own[:, D:]
    k_copy.wait()
    v_copy.wait()
    keys = k_ref[...].reshape(npos, D)
    values = v_ref[...].reshape(npos, 2 * D)
    nt = (((1,), (1,)), ((), ()))
    before = None
    width = 1024
    for h in range(heads + 1):
        top = acc = None
        for w in range(0, npos, width):
            if h < heads:
                s = lax.dot_general(q_of(h), keys[w : w + width], nt, preferred_element_type=F32)
                s = s * scale + bias_ref[:, w : w + width]
                s_ref[h % 2, :, w : w + width] = s
                for lane in range(0, width, 128):
                    part = s[:, lane : lane + 128]
                    top = part if top is None else jnp.maximum(top, part)
            if h:
                p = jnp.exp2(s_ref[(h - 1) % 2, :, w : w + width] - before[1]).astype(BF16)
                part = jnp.dot(p, values[w : w + width], preferred_element_type=F32)
                acc = part if acc is None else acc + part
        if h:
            own_w = jnp.exp2(before[0] - before[1])
            out = (acc[:, :D] + own_w * own_v) / (acc[:, D : D + 1] + own_w)
            store(h - 1, out.astype(BF16))
        if h < heads:
            own_s = jnp.sum(q_of(h).astype(F32) * own_k, axis=1, keepdims=True) * scale
            before = own_s, jnp.maximum(jnp.max(top, axis=1, keepdims=True), own_s)


def weight_copies(w_ref, held, sems, blocks):
    width = held.shape[2]
    out = []
    for i, block in enumerate(blocks):
        start = pl.multiple_of(block * width, width)
        out.append(pltpu.make_async_copy(w_ref.at[:, pl.ds(start, width)], held.at[i], sems.at[i]))
    return out


def chip_blocks(t, chips):
    chip, core = t // 2, t % 2
    out = []
    for d in range(1, chips):
        at = 2 * lax.rem(chip + d, chips)
        out += [at + 1 - core, at + core]
    return out


def attend_kernel(chips, members, leave_ref, recv_ref, q_ref, fresh_ref, idx_ref, len_ref, id_ref, pool_ref,
                  w_ref, attn_ref, *rest):
    sends, keeps, rest = rest[: len(RUNS)], rest[len(RUNS) : 2 * len(RUNS)], rest[2 * len(RUNS) :]
    half = members // 2
    evens, odd, (k_ref, v_ref, fresh, bias, s, held, psem, wsem) = rest[:half], rest[half], rest[half + 1 :]
    t, z = lax.axis_index("tensor"), lax.axis_index("replica")
    D = HEAD_SIZE
    rows, channels = attn_ref.shape
    kv = t * (channels // D) // (QUERY_HEADS_HALF // KVH)
    at = pl.multiple_of(kv * 2 * D, 2 * D)
    own_copy = pltpu.make_async_copy(fresh_ref.at[:, pl.ds(at, 2 * D)], fresh, psem.at[2])
    own_copy.start()
    copies = weight_copies(w_ref, held, wsem, chip_blocks(t, chips))

    def own_of():
        for c in copies:
            c.start()
        own_copy.wait()
        return fresh[...]

    def store(h, out):
        attn_ref[:, h * D : (h + 1) * D] = out

    attend(lambda h: q_ref[:, h * D : (h + 1) * D], own_of, idx_ref[...].astype(F32),
           len_ref[...].astype(F32), pool_ref, at, k_ref, v_ref, psem, bias, s, channels // D, store)
    a = attn_ref[...]
    width = held.shape[2]
    for i, c in enumerate(copies):
        c.wait()
        lo = (i // 2) * width
        out = jnp.dot(a, held[i], preferred_element_type=F32).astype(BF16)
        row = 0
        for ref in (sends, keeps)[i % 2]:
            ref[:, lo : lo + width] = out[row : row + ref.shape[0]]
            row += ref.shape[0]
    moved = leave_ref.shape[1]
    lane = lax.broadcasted_iota(jnp.int32, (PAD, rows), 1)
    row = lax.broadcasted_iota(jnp.int32, (PAD, rows), 0)
    pick = jnp.zeros((PAD, rows), jnp.bool_)
    for j in range(moved):
        pick = pick | ((row == j) & (lane == leave_ref[0, j]))
    pick = jnp.where(pick, 1.0, 0.0).astype(BF16)
    left = jnp.dot(pick, a, preferred_element_type=F32)
    nt = (((1,), (1,)), ((), ()))
    ids = jnp.broadcast_to(id_ref[...].astype(F32), (IDS, rows)).astype(BF16)
    id_col = lax.dot_general(pick, ids, nt, preferred_element_type=F32)
    left = jnp.concatenate([left, id_col], 1).astype(BF16)
    for k in range(members):
        pay = jnp.where(recv_ref[0] == (z ^ k), left, jnp.zeros_like(left))
        if k % 2:
            odd[PAD * (k // 2) : PAD * (k // 2 + 1), :] = pay
        else:
            evens[k // 2][...] = pay


def own_kernel(chips, members, groups, slots_ref, leave_ref, w_ref, id_ref, attn_ref, *rest):
    arr_ref, own_down, rest = rest[0], rest[1], rest[2:]
    same, swapped, rest = rest[: members - 1], rest[members - 1 : 2 * (members - 1)], rest[2 * (members - 1) :]
    send1, send2, own_ref, pack_send, pack_keep, slot_ref, fixed, held, wsem = rest
    t, z, y = lax.axis_index("tensor"), lax.axis_index("replica"), lax.axis_index("groups")
    copies = weight_copies(w_ref, held, wsem, [t + 1 - 2 * (t % 2), t] + chip_blocks(t, chips))
    for c in copies:
        c.start()
    rows, channels = fixed.shape
    moved = leave_ref.shape[1]
    arr = arr_ref[...]
    row = lax.broadcasted_iota(jnp.int32, (rows, channels), 0)
    whole = attn_ref[...].astype(F32)
    for j in range(moved):
        whole = jnp.where(row == leave_ref[0, j], arr[j : j + 1, :channels].astype(F32), whole)
    fixed[...] = whole.astype(BF16)
    ids = down_rows(id_ref[...].astype(F32))
    came = arr[:, channels:].astype(F32)
    row = lax.broadcasted_iota(jnp.int32, ids.shape, 0)
    for j in range(moved):
        ids = jnp.where(row == leave_ref[0, j], came[j : j + 1, 0:1], ids)
    slot = jnp.zeros_like(ids)
    for i in range(slots_ref.shape[0]):
        slot = jnp.where(ids == i, slots_ref[i].astype(F32), slot)
    slot_ref[...] = slot
    a = fixed[...]
    rank = own_down.shape[1]
    nt = (((1,), (1,)), ((), ()))
    slot = slot[:, : 2 * rank]
    total = jnp.zeros((rows, 2 * rank), F32)
    left = lax.broadcasted_iota(jnp.int32, total.shape, 1) < rank
    pieces = slot_pieces(members, groups, z, y, own_down, same, swapped)
    for (one, one_at), (two, two_at) in zip(pieces[::2], pieces[1::2]):
        part = lax.dot_general(a, jnp.concatenate([one, two], 0), nt, preferred_element_type=F32)
        total += jnp.where(slot == jnp.where(left, one_at, two_at).astype(F32), part, 0.0)
    shr = total[:, :rank] + total[:, rank:]
    shr = jnp.concatenate([shr, jnp.zeros((rows, 128 - rank), F32)], 1).astype(BF16)
    half = rows // 2
    copies[0].wait()
    send1[...] = jnp.dot(a[:half], held[0], preferred_element_type=F32).astype(BF16)
    send2[...] = jnp.dot(a[half:], held[0], preferred_element_type=F32).astype(BF16)
    copies[1].wait()
    own_ref[...] = jnp.dot(a, held[1], preferred_element_type=F32).astype(BF16)
    width = held.shape[2]
    for i, c in enumerate(copies[2:]):
        c.wait()
        pack = (pack_send, pack_keep)[i % 2]
        out = jnp.dot(arr[:, :channels], held[2 + i], preferred_element_type=F32).astype(BF16)
        parts = [out[:, c : c + 128] for c in range(0, width, 128)]
        lo, size = (i // 2) * rows, PAD * len(parts)
        pack[lo : lo + size, :128] = jnp.concatenate(parts, 0)
        if size < rows:
            pack[lo + size : lo + rows, :128] = jnp.zeros((rows - size, 128), BF16)
        pack[lo : lo + rows, 128:] = shr


def slice_kernel(down_ref, up_ref, down_out, up_out):
    y = lax.axis_index("groups")
    down_out[...] = down_ref[y]
    up_out[...] = up_ref[y]


def slot_pieces(members, groups, z, y, own, same, swapped):
    pieces = [(own[g], z * groups + g) for g in range(groups)]
    for k in range(1, members):
        layer = (z ^ k) * groups
        pieces.append((same[k - 1][...], layer + y))
        pieces.append((swapped[k - 1][...], layer + 1 - y))
    return pieces


def final_kernel(members, groups, chips, leave_ref, slot_ref, own_ref, got1, got2, own_up, *rest):
    same, swapped = rest[: members - 1], rest[members - 1 : 2 * (members - 1)]
    rest = rest[2 * (members - 1) :]
    packs, rest = rest[:chips], rest[chips:]
    moves, far, out_ref = rest[: chips - 1], rest[chips - 1 : -1], rest[-1]
    z, y = lax.axis_index("replica"), lax.axis_index("groups")
    rank = own_up.shape[1]
    shrunk = sum(p[:, 128 : 128 + rank].astype(F32) for p in packs)
    shrunk = shrunk.astype(BF16).astype(F32)
    wide = jnp.concatenate([shrunk, shrunk], 1)
    slot = slot_ref[:, : 2 * rank]
    left = lax.broadcasted_iota(jnp.int32, wide.shape, 1) < rank
    delta = None
    pieces = slot_pieces(members, groups, z, y, own_up, same, swapped)
    for (one, one_at), (two, two_at) in zip(pieces[::2], pieces[1::2]):
        spread = jnp.where(slot == jnp.where(left, one_at, two_at).astype(F32), wide, 0.0).astype(BF16)
        part = jnp.dot(spread, jnp.concatenate([one, two], 0), preferred_element_type=F32)
        delta = part if delta is None else delta + part
    got = jnp.concatenate([got1[...], got2[...]], 0)
    base = own_ref[...].astype(F32) + got.astype(F32) + ADAPTER_SCALE * delta
    others = jnp.concatenate(
        [sum(r[...].astype(F32) for r in far[i : i + chips - 1]) for i in range(0, len(far), chips - 1)], 0
    )
    came = sum(r[...].astype(F32) for r in moves)
    row = lax.broadcasted_iota(jnp.int32, base.shape, 0)
    for j in range(leave_ref.shape[1]):
        new = jnp.concatenate([came[c + j : c + j + 1, :] for c in range(0, came.shape[0], PAD)], 1)
        others = jnp.where(row == leave_ref[0, j], new, others)
    out_ref[...] = (base + others).astype(BF16)


def after(value, *others):
    return lax.optimization_barrier((value,) + others)[0]


def on_device(mesh_shape, queries, fresh, pool, table, lengths, adapter_id, storage_slot, leaving, receiving,
              w, down, up):
    members, tensors, groups = mesh_shape["replica"], mesh_shape["tensor"], mesh_shape["groups"]
    chips = tensors // 2
    rows, channels = queries.shape
    nblk, bs, _ = pool.shape
    npos = nblk * bs
    cols = w.shape[1] // tensors
    rank = down.shape[2]
    idx_t = table.T
    len_row = lengths[None, :]
    id_row = adapter_id[None, :]
    down_t = jnp.swapaxes(down, 1, 2)

    def across(v, k):
        return lax.ppermute(v, "replica", [(i, i ^ k) for i in range(members)])

    def swap(v):
        return lax.ppermute(v, "groups", [(0, 1), (1, 0)])

    def core(v):
        return lax.ppermute(v, "tensor", [(i, i ^ 1) for i in range(tensors)])

    def chip(v, d):
        return lax.ppermute(v, "tensor", [(i, (i + 2 * d) % tensors) for i in range(tensors)])

    def to_chips(v):
        return [chip(v[:, (d - 1) * cols : d * cols] if chips > 2 else v, d) for d in range(1, chips)]

    mine_down, mine_up = call(
        slice_kernel,
        [jax.ShapeDtypeStruct(v.shape[1:], BF16) for v in (down_t, up)],
        [VMEM, VMEM],
        [],
        "slices_of_this_group",
        (down_t, up),
        0,
    )

    def near(v):
        return {1 << i: across(v, 1 << i) for i in reversed(range(members.bit_length() - 1))}

    def passed(v, have):
        have = {0: v, **have}
        bit = members // 2
        while bit:
            for k in [k for k in have if k % (2 * bit) == 0 and k ^ bit not in have]:
                have[k ^ bit] = across(have[k], bit)
            bit //= 2
        return [have[k] for k in range(1, members)]

    down_near = near(mine_down)
    up_near = near(mine_up)
    sds = jax.ShapeDtypeStruct
    dma = pltpu.SemaphoreType.DMA
    far = (chips - 1) * cols
    sizes = [rows * r // sum(RUNS) for r in RUNS]
    attn, *out = call(
        functools.partial(attend_kernel, chips, members),
        [sds((rows, channels), BF16)] + [sds((n, far), BF16) for n in sizes] * 2
        + [sds((PAD, channels + IDS), BF16)] * (members // 2) + [sds((PAD * members // 2, channels + IDS), BF16)],
        [SMEM, SMEM, VMEM, ANY, VMEM, VMEM, VMEM, ANY, ANY],
        [
            pltpu.VMEM((nblk, bs, HEAD_SIZE), BF16),
            pltpu.VMEM((nblk, bs, 2 * HEAD_SIZE), BF16),
            pltpu.VMEM((rows, 2 * HEAD_SIZE), BF16),
            pltpu.VMEM((rows, npos), F32),
            pltpu.VMEM((2, rows, npos), F32),
            pltpu.VMEM((2 * (chips - 1), channels, cols), BF16),
            dma((3,)),
            dma((2 * (chips - 1),)),
        ],
        "attend_and_project",
        (leaving, receiving, queries, fresh, idx_t, len_row, id_row, pool, w),
        LONG,
    )
    runs = len(RUNS)
    sends, keeps, pays, odd = out[:runs], out[runs : 2 * runs], out[2 * runs : -1], out[-1]
    first = across(odd, 1)
    sends[0] = after(sends[0], *down_near.values(), *up_near.values())
    down_same = passed(mine_down, {k: after(v, attn) for k, v in down_near.items()})
    down_swapped = {k: swap(after(v, attn)) for k, v in down_near.items()}
    totals = [
        after(keep, first, *down_same, *down_swapped.values()) + core(send) for send, keep in zip(sends, keeps)
    ]
    pays = [pay + first[PAD * i : PAD * (i + 1)] for i, pay in enumerate(pays)]
    bit = 2
    while len(pays) > 1:
        got = across(jnp.concatenate(pays[1::2], 0), bit)
        pays = [pay + got[PAD * i : PAD * (i + 1)] for i, pay in enumerate(pays[::2])]
        bit *= 2
    arrived = pays
    x_in = [to_chips(total) for total in totals]
    up_same = passed(mine_up, {k: after(v, *arrived) for k, v in up_near.items()})
    down_swapped = [down_swapped[k + 1] if k + 1 in down_swapped else swap(after(v, *totals)) for k, v in enumerate(down_same)]
    up_swapped = {k: swap(after(v, *down_swapped, *arrived)) for k, v in up_near.items()}
    for k in range(1, members):
        if k not in up_swapped:
            up_swapped[k] = swap(up_same[k - 1])
    up_swapped = [up_swapped[k] for k in range(1, members)]
    send_own1, send_own2, own, pack_send, pack_keep, slot = call(
        functools.partial(own_kernel, chips, members, groups),
        [sds((rows // 2, cols), BF16)] * 2 + [sds((rows, cols), BF16)] + [sds(((chips - 1) * rows, 256), BF16)] * 2
        + [sds((rows, 128), F32)],
        [SMEM, SMEM, ANY, VMEM, VMEM] + [VMEM] * (2 + 2 * (members - 1)),
        [pltpu.VMEM((rows, channels), BF16), pltpu.VMEM((tensors, channels, cols), BF16), dma((tensors,))],
        "project_own_columns",
        (storage_slot, leaving, w, id_row, after(attn, *totals), *arrived, down_t, *down_same,
         *down_swapped),
        0,
    )
    got_own = [core(send_own1), core(send_own2)]
    pack = pack_keep + core(after(pack_send, *[up_swapped[k - 1] for k in up_near]))
    pack = after(pack, *x_in[0])
    packs = [pack[:rows]] + [chip(pack[(d - 1) * rows : d * rows], d) for d in range(1, chips)]

    tile = cols // 4
    col = lambda n: pl.BlockSpec((n, tile), lambda i: (0, i))
    still = lambda *shape: pl.BlockSpec(shape, lambda i: (0,) * len(shape))
    strip = pl.BlockSpec((PAD * tile // 128, 128), lambda i: (i, 0))
    return pl.pallas_call(
        functools.partial(final_kernel, members, groups, chips),
        grid=(cols // tile,),
        out_shape=sds((rows, cols), BF16),
        in_specs=[SMEM, still(rows, 128), col(rows), col(rows // 2), col(rows // 2),
                  pl.BlockSpec((groups, rank, tile), lambda i: (0, 0, i))]
        + [col(rank)] * (2 * (members - 1)) + [still(rows, 256)] * chips + [strip] * (chips - 1)
        + [col(n) for n in sizes for _ in range(chips - 1)],
        out_specs=col(rows),
        compiler_params=pltpu.CompilerParams(vmem_limit_bytes=VMEM_LIMIT),
        cost_estimate=cost(5),
        name="combine",
    )(leaving, slot, own, *got_own, up, *up_same, *up_swapped, *packs, *packs[1:], *[v for x in x_in for v in x])


def solution(mesh):
    return jax.shard_map(
        functools.partial(on_device, dict(mesh.shape)),
        mesh=mesh,
        in_specs=(
            P(("groups", "replica"), "tensor"),
            P(("groups", "replica"), None),
            P(("groups", "replica"), None, None),
            P(("groups", "replica"), None),
            P(("groups", "replica")),
            P(("groups", "replica")),
            P(),
            P(("groups", "replica"), None),
            P(("groups", "replica")),
            P("tensor", None),
            P("replica", "tensor", None),
            P("replica", None, "tensor"),
        ),
        out_specs=P(("groups", "replica"), "tensor"),
        check_vma=False,
    )
```

```python
import functools
import math

import jax
import jax.numpy as jnp
from jax import lax
from jax.experimental import pallas as pl
from jax.experimental.pallas import tpu as pltpu
from jax.sharding import PartitionSpec as P

QUERY_HEADS_HALF = 32
KVH = 4
HEAD_SIZE = 128
ADAPTER_SCALE = 2.0
RUNS = (1,)
LONG = 200
PAD = 16
IDS = 128
VMEM_LIMIT = 60 * 1024 * 1024
BF16 = jnp.bfloat16
F32 = jnp.float32
ANY = pl.BlockSpec(memory_space=pl.ANY)
VMEM = pl.BlockSpec(memory_space=pltpu.VMEM)
SMEM = pl.BlockSpec(memory_space=pltpu.SMEM)


def cost(micros):
    return pl.CostEstimate(flops=int(micros * 1.15e9), bytes_accessed=1024, transcendentals=0)


def call(body, out_shape, in_specs, scratch, name, args, micros, limit=VMEM_LIMIT):
    return pl.pallas_call(
        body,
        out_shape=out_shape,
        in_specs=in_specs,
        out_specs=[VMEM] * len(out_shape),
        scratch_shapes=scratch,
        compiler_params=pltpu.CompilerParams(vmem_limit_bytes=limit),
        cost_estimate=cost(micros),
        name=name,
    )(*args)


def down_rows(lane_row):
    return jnp.broadcast_to(lane_row, (128, lane_row.shape[1])).T


def attend(q_of, own_of, idx, lens, pool_ref, at, k_ref, v_ref, sems, bias_ref, s_ref, heads, store, begin):
    rows = idx.shape[1]
    D = HEAD_SIZE
    nblk, bs, _ = pool_ref.shape
    npos = nblk * bs
    scale = math.log2(math.e) / math.sqrt(D)
    k_copy = pltpu.make_async_copy(pool_ref.at[:, :, pl.ds(at, D)], k_ref, sems.at[0])
    v_copy = pltpu.make_async_copy(
        pool_ref.at[:, :, pl.ds(pl.multiple_of(at + D, D), D)], v_ref.at[:, :, pl.ds(0, D)], sems.at[1]
    )
    k_copy.start()
    v_copy.start()
    v_ref[:, :, D:] = jnp.ones((nblk, bs, D), BF16)
    nfull = jnp.floor(lens * (1.0 / bs))
    rem = lens - nfull * bs
    block = lax.broadcasted_iota(jnp.int32, (nblk, rows), 0).astype(F32)
    full = jnp.zeros((nblk, rows), F32)
    some = jnp.zeros((nblk, rows), F32)
    for j in range(idx.shape[0]):
        hit = idx[j : j + 1, :] == block
        full += jnp.where(hit & (nfull > j), 1.0, 0.0)
        some += jnp.where(hit & (lens > j * bs), 1.0, 0.0)
    full = full.astype(BF16)
    some = some.astype(BF16)
    width = 512
    offset = (lax.broadcasted_iota(jnp.int32, (rows, 128), 1) % bs).astype(F32)
    partial = jnp.concatenate([offset < down_rows(rem)] * (width // 128), 1)
    over_rows = (((0,), (0,)), ((), ()))
    for w in range(0, npos, width):
        spot = lax.broadcasted_iota(jnp.int32, (nblk, width), 1) + w
        here = spot // bs == lax.broadcasted_iota(jnp.int32, (nblk, width), 0)
        spread = jnp.where(here, 1.0, 0.0).astype(BF16)
        count_full = lax.dot_general(full, spread, over_rows, preferred_element_type=F32)
        count_some = lax.dot_general(some, spread, over_rows, preferred_element_type=F32)
        count = jnp.where(partial, count_some, count_full)
        bias_ref[:, w : w + width] = jnp.where(
            count > 0.5, jnp.log2(jnp.maximum(count, 1.0)), -jnp.inf
        )
    own = own_of().astype(F32)
    own_k, own_v = own[:, :D], own[:, D:]
    k_copy.wait()
    keys = k_ref[...].reshape(npos, D)
    nt = (((1,), (1,)), ((), ()))
    before = None
    width = 1024
    for h in range(heads + 1):
        top = acc = None
        if h == 1:
            v_copy.wait()
            begin()
            values = v_ref[...].reshape(npos, 2 * D)
        for w in range(0, npos, width):
            if h < heads:
                s = lax.dot_general(q_of(h), keys[w : w + width], nt, preferred_element_type=F32)
                s = s * scale + bias_ref[:, w : w + width]
                s_ref[h % 2, :, w : w + width] = s
                for lane in range(0, width, 128):
                    part = s[:, lane : lane + 128]
                    top = part if top is None else jnp.maximum(top, part)
            if h:
                p = jnp.exp2(s_ref[(h - 1) % 2, :, w : w + width] - before[1]).astype(BF16)
                part = jnp.dot(p, values[w : w + width], preferred_element_type=F32)
                acc = part if acc is None else acc + part
        if h:
            own_w = jnp.exp2(before[0] - before[1])
            out = (acc[:, :D] + own_w * own_v) / (acc[:, D : D + 1] + own_w)
            store(h - 1, out.astype(BF16))
        if h < heads:
            own_s = jnp.sum(q_of(h).astype(F32) * own_k, axis=1, keepdims=True) * scale
            before = own_s, jnp.maximum(jnp.max(top, axis=1, keepdims=True), own_s)


def weight_copies(w_ref, held, sems, blocks):
    width = held.shape[2]
    out = []
    for i, block in enumerate(blocks):
        start = pl.multiple_of(block * width, width)
        out.append(pltpu.make_async_copy(w_ref.at[:, pl.ds(start, width)], held.at[i], sems.at[i]))
    return out


def chip_blocks(t, chips):
    chip, core = t // 2, t % 2
    out = []
    for d in range(1, chips):
        at = 2 * lax.rem(chip + d, chips)
        out += [at + 1 - core, at + core]
    return out


def attend_kernel(chips, members, leave_ref, recv_ref, q_ref, fresh_ref, idx_ref, len_ref, id_ref, pool_ref,
                  w_ref, attn_ref, *rest):
    sends, keeps, rest = rest[: len(RUNS)], rest[len(RUNS) : 2 * len(RUNS)], rest[2 * len(RUNS) :]
    half = members // 2
    evens, odd, (k_ref, v_ref, fresh, bias, s, held, psem, wsem) = rest[:half], rest[half], rest[half + 1 :]
    t, z = lax.axis_index("tensor"), lax.axis_index("replica")
    D = HEAD_SIZE
    rows, channels = attn_ref.shape
    kv = t * (channels // D) // (QUERY_HEADS_HALF // KVH)
    at = pl.multiple_of(kv * 2 * D, 2 * D)
    own_copy = pltpu.make_async_copy(fresh_ref.at[:, pl.ds(at, 2 * D)], fresh, psem.at[2])
    own_copy.start()
    copies = weight_copies(w_ref, held, wsem, chip_blocks(t, chips))

    def own_of():
        own_copy.wait()
        return fresh[...]

    def begin():
        for c in copies:
            c.start()

    def store(h, out):
        attn_ref[:, h * D : (h + 1) * D] = out

    attend(lambda h: q_ref[:, h * D : (h + 1) * D], own_of, idx_ref[...].astype(F32),
           len_ref[...].astype(F32), pool_ref, at, k_ref, v_ref, psem, bias, s, channels // D, store, begin)
    a = attn_ref[...]
    width = held.shape[2]
    for i, c in enumerate(copies):
        c.wait()
        lo = (i // 2) * width
        out = jnp.dot(a, held[i], preferred_element_type=F32).astype(BF16)
        row = 0
        for ref in (sends, keeps)[i % 2]:
            ref[:, lo : lo + width] = out[row : row + ref.shape[0]]
            row += ref.shape[0]
    moved = leave_ref.shape[1]
    lane = lax.broadcasted_iota(jnp.int32, (PAD, rows), 1)
    row = lax.broadcasted_iota(jnp.int32, (PAD, rows), 0)
    pick = jnp.zeros((PAD, rows), jnp.bool_)
    for j in range(moved):
        pick = pick | ((row == j) & (lane == leave_ref[0, j]))
    pick = jnp.where(pick, 1.0, 0.0).astype(BF16)
    left = jnp.dot(pick, a, preferred_element_type=F32)
    nt = (((1,), (1,)), ((), ()))
    ids = jnp.broadcast_to(id_ref[...].astype(F32), (IDS, rows)).astype(BF16)
    id_col = lax.dot_general(pick, ids, nt, preferred_element_type=F32)
    left = jnp.concatenate([left, id_col], 1).astype(BF16)
    for k in range(members):
        pay = jnp.where(recv_ref[0] == (z ^ k), left, jnp.zeros_like(left))
        if k % 2:
            odd[PAD * (k // 2) : PAD * (k // 2 + 1), :] = pay
        else:
            evens[k // 2][...] = pay


def own_kernel(chips, members, groups, slots_ref, leave_ref, w_ref, id_ref, attn_ref, *rest):
    arr_ref, own_down, rest = rest[0], rest[1], rest[2:]
    same, swapped, rest = rest[: members - 1], rest[members - 1 : 2 * (members - 1)], rest[2 * (members - 1) :]
    send1, send2, own_ref, pack_send, pack_keep, slot_ref, fixed, held, wsem = rest
    t, z, y = lax.axis_index("tensor"), lax.axis_index("replica"), lax.axis_index("groups")
    copies = weight_copies(w_ref, held, wsem, [t + 1 - 2 * (t % 2), t] + chip_blocks(t, chips))
    for c in copies:
        c.start()
    rows, channels = fixed.shape
    moved = leave_ref.shape[1]
    arr = arr_ref[...]
    row = lax.broadcasted_iota(jnp.int32, (rows, channels), 0)
    whole = attn_ref[...].astype(F32)
    for j in range(moved):
        whole = jnp.where(row == leave_ref[0, j], arr[j : j + 1, :channels].astype(F32), whole)
    fixed[...] = whole.astype(BF16)
    ids = down_rows(id_ref[...].astype(F32))
    came = arr[:, channels:].astype(F32)
    row = lax.broadcasted_iota(jnp.int32, ids.shape, 0)
    for j in range(moved):
        ids = jnp.where(row == leave_ref[0, j], came[j : j + 1, 0:1], ids)
    slot = jnp.zeros_like(ids)
    for i in range(slots_ref.shape[0]):
        slot = jnp.where(ids == i, slots_ref[i].astype(F32), slot)
    slot_ref[...] = slot
    a = fixed[...]
    rank = own_down.shape[1]
    nt = (((1,), (1,)), ((), ()))
    slot = slot[:, : 2 * rank]
    total = jnp.zeros((rows, 2 * rank), F32)
    left = lax.broadcasted_iota(jnp.int32, total.shape, 1) < rank
    pieces = slot_pieces(members, groups, z, y, own_down, same, swapped)
    for (one, one_at), (two, two_at) in zip(pieces[::2], pieces[1::2]):
        part = lax.dot_general(a, jnp.concatenate([one, two], 0), nt, preferred_element_type=F32)
        total += jnp.where(slot == jnp.where(left, one_at, two_at).astype(F32), part, 0.0)
    shr = total[:, :rank] + total[:, rank:]
    shr = jnp.concatenate([shr, jnp.zeros((rows, 128 - rank), F32)], 1).astype(BF16)
    half = rows // 2
    copies[0].wait()
    send1[...] = jnp.dot(a[:half], held[0], preferred_element_type=F32).astype(BF16)
    send2[...] = jnp.dot(a[half:], held[0], preferred_element_type=F32).astype(BF16)
    copies[1].wait()
    own_ref[...] = jnp.dot(a, held[1], preferred_element_type=F32).astype(BF16)
    width = held.shape[2]
    for i, c in enumerate(copies[2:]):
        c.wait()
        pack = (pack_send, pack_keep)[i % 2]
        out = jnp.dot(arr[:, :channels], held[2 + i], preferred_element_type=F32).astype(BF16)
        parts = [out[:, c : c + 128] for c in range(0, width, 128)]
        lo, size = (i // 2) * rows, PAD * len(parts)
        pack[lo : lo + size, :128] = jnp.concatenate(parts, 0)
        if size < rows:
            pack[lo + size : lo + rows, :128] = jnp.zeros((rows - size, 128), BF16)
        pack[lo : lo + rows, 128:] = shr


def slice_kernel(down_ref, up_ref, down_out, up_out):
    y = lax.axis_index("groups")
    down_out[...] = down_ref[y]
    up_out[...] = up_ref[y]


def slot_pieces(members, groups, z, y, own, same, swapped):
    pieces = [(own[g], z * groups + g) for g in range(groups)]
    for k in range(1, members):
        layer = (z ^ k) * groups
        pieces.append((same[k - 1][...], layer + y))
        pieces.append((swapped[k - 1][...], layer + 1 - y))
    return pieces


def final_kernel(members, groups, chips, leave_ref, slot_ref, own_ref, got1, got2, own_up, *rest):
    same, swapped = rest[: members - 1], rest[members - 1 : 2 * (members - 1)]
    rest = rest[2 * (members - 1) :]
    packs, rest = rest[:chips], rest[chips:]
    moves, far, out_ref = rest[: chips - 1], rest[chips - 1 : -1], rest[-1]
    z, y = lax.axis_index("replica"), lax.axis_index("groups")
    rank = own_up.shape[1]
    shrunk = sum(p[:, 128 : 128 + rank].astype(F32) for p in packs)
    shrunk = shrunk.astype(BF16).astype(F32)
    wide = jnp.concatenate([shrunk, shrunk], 1)
    slot = slot_ref[:, : 2 * rank]
    left = lax.broadcasted_iota(jnp.int32, wide.shape, 1) < rank
    delta = None
    pieces = slot_pieces(members, groups, z, y, own_up, same, swapped)
    for (one, one_at), (two, two_at) in zip(pieces[::2], pieces[1::2]):
        spread = jnp.where(slot == jnp.where(left, one_at, two_at).astype(F32), wide, 0.0).astype(BF16)
        part = jnp.dot(spread, jnp.concatenate([one, two], 0), preferred_element_type=F32)
        delta = part if delta is None else delta + part
    got = jnp.concatenate([got1[...], got2[...]], 0)
    base = own_ref[...].astype(F32) + got.astype(F32) + ADAPTER_SCALE * delta
    others = jnp.concatenate(
        [sum(r[...].astype(F32) for r in far[i : i + chips - 1]) for i in range(0, len(far), chips - 1)], 0
    )
    came = sum(r[...].astype(F32) for r in moves)
    row = lax.broadcasted_iota(jnp.int32, base.shape, 0)
    for j in range(leave_ref.shape[1]):
        new = jnp.concatenate([came[c + j : c + j + 1, :] for c in range(0, came.shape[0], PAD)], 1)
        others = jnp.where(row == leave_ref[0, j], new, others)
    out_ref[...] = (base + others).astype(BF16)


def after(value, *others):
    return lax.optimization_barrier((value,) + others)[0]


def on_device(mesh_shape, queries, fresh, pool, table, lengths, adapter_id, storage_slot, leaving, receiving,
              w, down, up):
    members, tensors, groups = mesh_shape["replica"], mesh_shape["tensor"], mesh_shape["groups"]
    chips = tensors // 2
    rows, channels = queries.shape
    nblk, bs, _ = pool.shape
    npos = nblk * bs
    cols = w.shape[1] // tensors
    rank = down.shape[2]
    idx_t = table.T
    len_row = lengths[None, :]
    id_row = adapter_id[None, :]
    down_t = jnp.swapaxes(down, 1, 2)

    def across(v, k):
        return lax.ppermute(v, "replica", [(i, i ^ k) for i in range(members)])

    def swap(v):
        return lax.ppermute(v, "groups", [(0, 1), (1, 0)])

    def core(v):
        return lax.ppermute(v, "tensor", [(i, i ^ 1) for i in range(tensors)])

    def chip(v, d):
        return lax.ppermute(v, "tensor", [(i, (i + 2 * d) % tensors) for i in range(tensors)])

    def to_chips(v):
        return [chip(v[:, (d - 1) * cols : d * cols] if chips > 2 else v, d) for d in range(1, chips)]

    mine_down, mine_up = call(
        slice_kernel,
        [jax.ShapeDtypeStruct(v.shape[1:], BF16) for v in (down_t, up)],
        [VMEM, VMEM],
        [],
        "slices_of_this_group",
        (down_t, up),
        0,
    )

    def near(v):
        return {1 << i: across(v, 1 << i) for i in reversed(range(members.bit_length() - 1))}

    def passed(v, have):
        have = {0: v, **have}
        bit = members // 2
        while bit:
            for k in [k for k in have if k % (2 * bit) == 0 and k ^ bit not in have]:
                have[k ^ bit] = across(have[k], bit)
            bit //= 2
        return [have[k] for k in range(1, members)]

    down_near = near(mine_down)
    up_near = near(mine_up)
    sds = jax.ShapeDtypeStruct
    dma = pltpu.SemaphoreType.DMA
    far = (chips - 1) * cols
    sizes = [rows * r // sum(RUNS) for r in RUNS]
    attn, *out = call(
        functools.partial(attend_kernel, chips, members),
        [sds((rows, channels), BF16)] + [sds((n, far), BF16) for n in sizes] * 2
        + [sds((PAD, channels + IDS), BF16)] * (members // 2) + [sds((PAD * members // 2, channels + IDS), BF16)],
        [SMEM, SMEM, VMEM, ANY, VMEM, VMEM, VMEM, ANY, ANY],
        [
            pltpu.VMEM((nblk, bs, HEAD_SIZE), BF16),
            pltpu.VMEM((nblk, bs, 2 * HEAD_SIZE), BF16),
            pltpu.VMEM((rows, 2 * HEAD_SIZE), BF16),
            pltpu.VMEM((rows, npos), F32),
            pltpu.VMEM((2, rows, npos), F32),
            pltpu.VMEM((2 * (chips - 1), channels, cols), BF16),
            dma((3,)),
            dma((2 * (chips - 1),)),
        ],
        "attend_and_project",
        (leaving, receiving, queries, fresh, idx_t, len_row, id_row, pool, w),
        LONG,
    )
    runs = len(RUNS)
    sends, keeps, pays, odd = out[:runs], out[runs : 2 * runs], out[2 * runs : -1], out[-1]
    first = across(odd, 1)
    sends[0] = after(sends[0], *down_near.values(), *up_near.values())
    down_same = passed(mine_down, {k: after(v, attn) for k, v in down_near.items()})
    down_swapped = {k: swap(after(v, attn)) for k, v in down_near.items()}
    totals = [after(keep, first) + core(send) for send, keep in zip(sends, keeps)]
    pays = [pay + first[PAD * i : PAD * (i + 1)] for i, pay in enumerate(pays)]
    bit = 2
    while len(pays) > 1:
        got = after(across(after(jnp.concatenate(pays[1::2], 0), *totals), bit), *down_same, *down_swapped.values())
        pays = [pay + got[PAD * i : PAD * (i + 1)] for i, pay in enumerate(pays[::2])]
        bit *= 2
    arrived = pays
    x_in = [to_chips(total) for total in totals]
    up_same = passed(mine_up, {k: after(v, *arrived) for k, v in up_near.items()})
    down_swapped = [down_swapped[k + 1] if k + 1 in down_swapped else swap(after(v, *totals)) for k, v in enumerate(down_same)]
    up_swapped = {k: swap(after(v, *down_swapped, *arrived)) for k, v in up_near.items()}
    for k in range(1, members):
        if k not in up_swapped:
            up_swapped[k] = swap(up_same[k - 1])
    up_swapped = [up_swapped[k] for k in range(1, members)]
    send_own1, send_own2, own, pack_send, pack_keep, slot = call(
        functools.partial(own_kernel, chips, members, groups),
        [sds((rows // 2, cols), BF16)] * 2 + [sds((rows, cols), BF16)] + [sds(((chips - 1) * rows, 256), BF16)] * 2
        + [sds((rows, 128), F32)],
        [SMEM, SMEM, ANY, VMEM, VMEM] + [VMEM] * (2 + 2 * (members - 1)),
        [pltpu.VMEM((rows, channels), BF16), pltpu.VMEM((tensors, channels, cols), BF16), dma((tensors,))],
        "project_own_columns",
        (storage_slot, leaving, w, id_row, after(attn, *totals), *arrived, down_t, *down_same,
         *down_swapped),
        0,
    )
    got_own = [core(send_own1), core(send_own2)]
    pack = pack_keep + core(after(pack_send, *[up_swapped[k - 1] for k in up_near]))
    pack = after(pack, *x_in[0])
    packs = [pack[:rows]] + [chip(pack[(d - 1) * rows : d * rows], d) for d in range(1, chips)]

    tile = cols // 2
    col = lambda n: pl.BlockSpec((n, tile), lambda i: (0, i))
    still = lambda *shape: pl.BlockSpec(shape, lambda i: (0,) * len(shape))
    strip = pl.BlockSpec((PAD * tile // 128, 128), lambda i: (i, 0))
    return pl.pallas_call(
        functools.partial(final_kernel, members, groups, chips),
        grid=(cols // tile,),
        out_shape=sds((rows, cols), BF16),
        in_specs=[SMEM, still(rows, 128), col(rows), col(rows // 2), col(rows // 2),
                  pl.BlockSpec((groups, rank, tile), lambda i: (0, 0, i))]
        + [col(rank)] * (2 * (members - 1)) + [still(rows, 256)] * chips + [strip] * (chips - 1)
        + [col(n) for n in sizes for _ in range(chips - 1)],
        out_specs=col(rows),
        compiler_params=pltpu.CompilerParams(vmem_limit_bytes=VMEM_LIMIT),
        cost_estimate=cost(5),
        name="combine",
    )(leaving, slot, own, *got_own, up, *up_same, *up_swapped, *packs, *packs[1:], *[v for x in x_in for v in x])


def solution(mesh):
    return jax.shard_map(
        functools.partial(on_device, dict(mesh.shape)),
        mesh=mesh,
        in_specs=(
            P(("groups", "replica"), "tensor"),
            P(("groups", "replica"), None),
            P(("groups", "replica"), None, None),
            P(("groups", "replica"), None),
            P(("groups", "replica")),
            P(("groups", "replica")),
            P(),
            P(("groups", "replica"), None),
            P(("groups", "replica")),
            P("tensor", None),
            P("replica", "tensor", None),
            P("replica", None, "tensor"),
        ),
        out_specs=P(("groups", "replica"), "tensor"),
        check_vma=False,
    )
```
